512 devices in a mesh: lat: 16 (over z_lo, core), lon: 32 (over z_hi, y, x).
Axes of the slice: x: 4, y: 4, z: 16 (z_hi: 2, z_lo: 8; z = z_hi * 8 + z_lo), core: 2. Of those that a mesh axis runs over, the one named last changes fastest.
Arguments:
- inputs: bfloat16 [128, 512, 256], P('lat', 'lon'), may hold values from -6 to 6
- out_grad: bfloat16 [128, 512, 256], P('lat', 'lon'), may hold values from -6 to 6
- weight: bfloat16 [9, 256, 256], replicated, may hold values from -0.125 to 0.125
- kernel_basis: bfloat16 [128, 9, 17, 33], P('lat'), may hold values from -0.25 to 0.25
- band_start: int32 [128], P('lat'), may hold values from 0 to 8, as said below
- band_width: int32 [128], P('lat'), may hold values from 1 to 17
- lon_reach: int32 [128], P('lat'), may hold values from 1 to 16
Outputs:
- output: bfloat16 [128, 512, 256], P('lat', 'lon')
- input_grad: bfloat16 [128, 512, 256], P('lat', 'lon')
- weight_grad: float32 [9, 256, 256], replicated
The draws below stay inside these ranges and needn't reach their ends.
Inputs may be any that keep to these rules, and one draw needn't show every extreme that they name: band_start + band_width <= 17 on every row.
All inputs are finite; a program needn't handle non-finite values.
Results may differ from the reference program's by a relative error of at most 0.0049.
Values may be sent and summed in bfloat16 or wider, within the bound.
A program may use at most 64 MiB of HBM per device.

```python
import math
import jax
import jax.numpy as jnp
from jax import lax

C = 256
K = 9
RAD = 8
HALO = 16
BAND = 17
LONW = 33
NLAT = 128
NLON = 512


def band_pair(key):
    key_start, key_width, key_full, key_edge = jax.random.split(key, 4)
    starts = jax.random.randint(key_start, (NLAT,), 0, RAD + 1)
    widths = 1 + jax.random.randint(key_width, (NLAT,), 0, 1 << 20) % (BAND - starts)
    full_row = jax.random.randint(key_full, (), 0, NLAT)
    edge_row = (full_row + 1 + jax.random.randint(key_edge, (), 0, NLAT - 1)) % NLAT
    row_ids = jnp.arange(NLAT)
    starts = jnp.where(row_ids == full_row, 0, jnp.where(row_ids == edge_row, RAD, starts))
    widths = jnp.where(row_ids == full_row, BAND, jnp.where(row_ids == edge_row, 1 + (widths - 1) % (RAD + 1), widths))
    return (starts.astype(jnp.int32), widths.astype(jnp.int32))


def draw_band_start(key, part):
    starts, widths = band_pair(key)
    return starts


def draw_band_width(key, part):
    starts, widths = band_pair(key)
    return widths


def draw_lon_reach(key, part):
    key = jax.random.fold_in(key, 7)
    key_reach, key_full = jax.random.split(key, 2)
    reach = jax.random.randint(key_reach, (NLAT,), 1, HALO + 1)
    full_row = jax.random.randint(key_full, (), 0, NLAT)
    return jnp.where(jnp.arange(NLAT) == full_row, HALO, reach).astype(jnp.int32)


def levels(rng, extent, cuts, least, high):
    def one(dim, parts):
        draws = jax.random.uniform(jax.random.fold_in(jax.random.fold_in(rng, 6), dim), (parts,), jnp.float32, least / len(cuts), high / len(cuts))
        return jnp.repeat(jnp.exp(draws), extent[dim] // parts).reshape((-1,) + (1,) * (len(extent) - dim - 1))

    level = one(*cuts[0])
    for cut in cuts[1:]:
        level = level * one(*cut)
    return level


def gaussian(key, extent, scale, limit, cuts=(), kind=jnp.bfloat16):
    entries = jax.random.normal(key, extent, jnp.float32) * scale
    if len(cuts) > 0:
        entries = levels(key, extent, cuts, -0.22, 0.18) * entries
    return jnp.clip(entries, min=-limit, max=limit).astype(kind)


def setup_inputs(seed: int = 0) -> dict:
    arg_keys = jax.random.split(jax.random.key(seed), 8)
    inputs = gaussian(arg_keys[0], (NLAT, NLON, C), 1.0, 6.0, ((0, 16), (1, 32)))
    out_grad = gaussian(arg_keys[1], (NLAT, NLON, C), 1.0, 6.0, ((0, 16), (1, 32)))
    weight = gaussian(arg_keys[2], (K, C, C), (K * C) ** -0.5, 0.125)
    kernel_basis = gaussian(arg_keys[3], (NLAT, K, BAND, LONW), (BAND * LONW) ** -0.5, 0.25, ((0, 16),))
    band_start = draw_band_start(jax.random.fold_in(arg_keys[7], 71), 0)
    band_width = draw_band_width(jax.random.fold_in(arg_keys[7], 71), 0)
    lon_reach = draw_lon_reach(jax.random.fold_in(arg_keys[7], 71), 0)
    return {"inputs": inputs, "out_grad": out_grad, "weight": weight, "kernel_basis": kernel_basis, "band_start": band_start, "band_width": band_width, "lon_reach": lon_reach}


def keep_basis(kernel_basis, band_start, band_width, lon_reach):
    band_size = kernel_basis.shape[2]
    lon_size = kernel_basis.shape[3]
    lon_middle = (lon_size - 1) // 2
    band_pos = jnp.arange(band_size, dtype=jnp.int32)[None, :, None]
    lon_pos = jnp.arange(lon_size, dtype=jnp.int32)[None, None, :]
    starts = band_start[:, None, None]
    inside = (band_pos >= starts) & (band_pos < starts + band_width[:, None, None])
    inside = inside & (jnp.abs(lon_pos - lon_middle) <= lon_reach[:, None, None])
    return jnp.where(inside[:, None], kernel_basis, jnp.zeros_like(kernel_basis))

def reference(inputs, out_grad, weight, kernel_basis, band_start, band_width, lon_reach):
    kept = keep_basis(kernel_basis, band_start, band_width, lon_reach).astype(jnp.float32)
    lon_index = (jnp.arange(LONW, dtype=jnp.int32) - HALO) % NLON
    cycle = jnp.zeros((NLAT, K, BAND, NLON), jnp.float32).at[:, :, :, lon_index].set(kept)
    cycle_freq = jnp.fft.rfft(cycle, axis=-1)
    padded_in = jnp.pad(inputs.astype(jnp.float32), ((RAD, RAD), (0, 0), (0, 0)))
    input_freq = jnp.fft.rfft(padded_in, axis=1)
    weight_wide = weight.astype(jnp.float32)
    grad_wide = out_grad.astype(jnp.float32)

    def row_step(carry, row_id):
        weight_acc, grad_freq = carry
        kernel_row = cycle_freq[row_id]
        window = lax.dynamic_slice_in_dim(input_freq, row_id, BAND, 0)
        mixed_freq = jnp.einsum('kbf,bfc->kfc', jnp.conj(kernel_row), window)
        mixed = jnp.fft.irfft(mixed_freq, n=NLON, axis=1).astype(jnp.bfloat16)
        mixed = lax.optimization_barrier(mixed).astype(jnp.float32)
        out_row = jnp.einsum('knc,koc->no', mixed, weight_wide).astype(jnp.bfloat16)
        grad_row = grad_wide[row_id]
        weight_acc = weight_acc + jnp.einsum('no,knc->koc', grad_row, mixed)
        back_row = jnp.einsum('no,koc->knc', grad_row, weight_wide).astype(jnp.bfloat16)
        back_row = lax.optimization_barrier(back_row).astype(jnp.float32)
        back_freq = jnp.fft.rfft(back_row, axis=1)
        contrib = jnp.einsum('kbf,kfc->bfc', kernel_row, back_freq)
        current = lax.dynamic_slice_in_dim(grad_freq, row_id, BAND, 0)
        grad_freq = lax.dynamic_update_slice_in_dim(grad_freq, current + contrib, row_id, 0)
        return ((weight_acc, grad_freq), out_row)
    start_carry = (jnp.zeros((K, C, C), jnp.float32), jnp.zeros((NLAT + 2 * RAD, NLON // 2 + 1, C), input_freq.dtype))
    (weight_acc, grad_freq), output = lax.scan(row_step, start_carry, jnp.arange(NLAT, dtype=jnp.int32))
    input_grad = jnp.fft.irfft(grad_freq[RAD:RAD + NLAT], n=NLON, axis=1).astype(jnp.bfloat16)
    weight_grad = weight_acc * (1.0 / math.sqrt(NLAT * NLON))
    return (output, input_grad, weight_grad)
```

```python
import functools
import math

import jax
import jax.numpy as jnp
from jax import lax
from jax.experimental import pallas as pl
from jax.experimental.pallas import tpu as pltpu
from jax.sharding import PartitionSpec as P

MESH = pl.DeviceIdType.MESH
F32, BF16 = jnp.float32, jnp.bfloat16

ROWS, COLS, CH = 8, 16, 256
CELLS = ROWS * COLS
K, BAND, LONW = 9, 17, 33
EXT = 3 * ROWS
PITCH = 64
FLAT = EXT * PITCH
PAIRS = EXT // 2
HALF = 128
GROUPS = 3
KG = K // GROUPS
SLICE = 16


def whole_wait(buf, sem):
    pltpu.make_async_copy(buf, buf, sem).wait()


def kernel(
    x_ref, g_ref, w_ref, kb_ref, start_ref, width_ref, reach_ref,
    out_ref, ig_ref, dw_ref,
    xh, kbs, comb, op, mg, mgt, mid, lat_out, lat_in, lon_out, lon_in,
    gt, gpeer, mfull, mm, msend, dws, rsb, zs, zb, zg, zgd, fin, dwv,
    xsend, xrecv, gsem, igsend, igrecv, msem_s, msem_r,
    rs_s, rs_r, z_s, z_r, zg_s, zg_r, fin_s, fin_r, ag_s, ag_r, fw_s, fw_r, loc,
):
    lat, lon = lax.axis_index("lat"), lax.axis_index("lon")
    core = lax.rem(lat, 2)
    zlo = lat // 2
    zhi = lon // 16
    rank = lax.rem(lon, 16)
    z4 = lax.rem(zlo, 4)
    zgroup = zhi * 2 + zlo // 4
    up, down = lat - 1, lat + 1
    has_up, has_down = lat > 0, lat < 15
    east, west = lax.rem(lon + 1, 32), lax.rem(lon + 31, 32)
    partner = (lat + 1 - 2 * core, lon)

    def plane_peer(d):
        return (lat, zhi * 16 + lax.rem(rank + d, 16))

    def z4_peer(t):
        return ((zlo - z4 + t) * 2 + core, lon)

    def zfar_peer(t):
        return (((t % 2) * 4 + z4) * 2 + core, (t // 2) * 16 + rank)

    def remote(src, dst, ssem, rsem, dev):
        return pltpu.make_async_remote_copy(
            src_ref=src, dst_ref=dst, send_sem=ssem, recv_sem=rsem, device_id=dev, device_id_type=MESH
        )

    xh[...] = jnp.zeros_like(xh)
    lat_in[...] = jnp.zeros_like(lat_in)

    bar = pltpu.get_barrier_semaphore()

    def signal(dev):
        pl.semaphore_signal(bar, inc=1, device_id=dev, device_id_type=MESH)

    signal((lat, east))
    signal((lat, west))
    for d in range(1, 4):
        signal(zfar_peer(lax.rem(zgroup + d, 4)))
    for d in range(1, 16):
        signal(plane_peer(d))
    for d in range(1, 4):
        signal(z4_peer(lax.rem(z4 + d, 4)))

    @pl.when(has_up)
    def _():
        signal((up, lon))

    @pl.when(has_down)
    def _():
        signal((down, lon))

    kbs[...] = jnp.zeros_like(kbs)
    band_pos = lax.broadcasted_iota(jnp.int32, (BAND, LONW), 0)
    lon_off = jnp.abs(lax.broadcasted_iota(jnp.int32, (BAND, LONW), 1) - (LONW - 1) // 2)

    xh[ROWS : 2 * ROWS, COLS : 2 * COLS, :] = x_ref[...]

    def op_step(k, carry):
        for i in range(ROWS):
            first = start_ref[i]
            inside = (band_pos >= first) & (band_pos < first + width_ref[i]) & (lon_off <= reach_ref[i])
            kbs[i, 1 : 1 + BAND, 0:LONW] = jnp.where(inside, kb_ref[i, k].astype(F32), 0.0)
            comb[i] = kbs[i, 0:24] + pltpu.roll(kbs[i, 1:25], PITCH, 1)
        for i in range(ROWS):
            for q in range(PAIRS):
                t = 2 * q - i + 1
                if 0 <= t <= BAND:
                    row = jnp.broadcast_to(comb[i, t : t + 1, :], (COLS, 128))
                    tile = pltpu.roll(row, 0, 1, stride=1, stride_axis=0)
                    op[k, i * COLS : (i + 1) * COLS, q * 128 : (q + 1) * 128] = tile.astype(BF16)
                else:
                    op[k, i * COLS : (i + 1) * COLS, q * 128 : (q + 1) * 128] = jnp.zeros((COLS, 128), BF16)
        return carry

    lax.fori_loop(0, K, op_step, 0)

    g = g_ref[...].reshape(CELLS, CH)

    def mg_step(k, carry):
        part = jnp.dot(g, w_ref[k], preferred_element_type=F32).astype(BF16)
        mg[k] = part.astype(F32).T.astype(BF16)
        return carry

    lax.fori_loop(0, K, mg_step, 0)
    for k in range(K):
        mgt[:, k * CELLS : (k + 1) * CELLS] = mg[k]
    gt[:, 0:CELLS] = g.astype(F32).T.astype(BF16)

    for n in range(FLAT // 256):
        part = jnp.dot(
            mgt[...], op[:, :, n * 256 : (n + 1) * 256].reshape(K * CELLS, 256), preferred_element_type=F32
        )
        part = part.T.reshape(4, PITCH, CH)[:, : 3 * COLS]
        r = n * 4
        if r < ROWS:
            lat_out[0, r : r + 4] = part.astype(BF16)
        elif r < 2 * ROWS:
            mid[r - ROWS : r - ROWS + 4] = part
        else:
            lat_out[1, r - 2 * ROWS : r - 2 * ROWS + 4] = part.astype(BF16)

    pl.semaphore_wait(bar, 23 + has_up.astype(jnp.int32) + has_down.astype(jnp.int32))

    mid_rows, top, bottom = pl.ds(ROWS, ROWS), pl.ds(0, ROWS), pl.ds(2 * ROWS, ROWS)
    mid_cols, wcols, ecols = pl.ds(COLS, COLS), pl.ds(0, COLS), pl.ds(2 * COLS, COLS)
    to_east = remote(x_ref, xh.at[mid_rows, wcols], xsend.at[0], xrecv.at[0], (lat, east))
    to_west = remote(x_ref, xh.at[mid_rows, ecols], xsend.at[1], xrecv.at[1], (lat, west))
    to_east.start()
    to_west.start()
    g_send = remote(g_ref, gpeer, gsem.at[0], gsem.at[1], partner)
    g_send.start()

    def up_down(cols, s):
        src = xh.at[mid_rows, cols]
        return (
            remote(src, xh.at[bottom, cols], xsend.at[s], xrecv.at[s], (up, lon)),
            remote(src, xh.at[top, cols], xsend.at[s + 1], xrecv.at[s + 1], (down, lon)),
        )

    verticals = (up_down(mid_cols, 2), up_down(wcols, 4), up_down(ecols, 6))
    ig_up = remote(lat_out.at[0], lat_in.at[1], igsend.at[0], igrecv.at[0], (up, lon))
    ig_down = remote(lat_out.at[1], lat_in.at[0], igsend.at[1], igrecv.at[1], (down, lon))

    def start_vertical(pair):
        @pl.when(has_up)
        def _():
            pair[0].start()

        @pl.when(has_down)
        def _():
            pair[1].start()

    def wait_vertical(pair):
        @pl.when(has_down)
        def _():
            pair[0].wait_recv()

        @pl.when(has_up)
        def _():
            pair[1].wait_recv()

    start_vertical(verticals[0])
    start_vertical((ig_up, ig_down))

    g_send.wait_recv()
    gt[:, CELLS : 2 * CELLS] = gpeer[...].reshape(CELLS, CH).astype(F32).T.astype(BF16)
    wait_vertical((ig_up, ig_down))
    total = mid[...] + lat_in[0].astype(F32) + lat_in[1].astype(F32)
    lon_out[0] = total[:, 0:COLS].astype(BF16)
    lon_out[1] = total[:, 2 * COLS : 3 * COLS].astype(BF16)
    mid[:, COLS : 2 * COLS] = total[:, COLS : 2 * COLS]
    ig_west = remote(lon_out.at[0], lon_in.at[1], igsend.at[2], igrecv.at[2], (lat, west))
    ig_east = remote(lon_out.at[1], lon_in.at[0], igsend.at[3], igrecv.at[3], (lat, east))

    to_east.wait_recv()
    start_vertical(verticals[1])
    to_west.wait_recv()
    start_vertical(verticals[2])
    ig_west.start()
    ig_east.start()
    for pair in verticals:
        wait_vertical(pair)

    flat_x = xh[...].reshape(FLAT, CH)
    m_copies = []
    for s in range(GROUPS):
        ks = pl.ds(s * KG, KG)
        m = jnp.dot(op[s * KG : (s + 1) * KG].reshape(KG * CELLS, FLAT), flat_x, preferred_element_type=F32)
        m = m.astype(BF16).reshape(KG, CELLS, CH)
        mfull[s * KG : (s + 1) * KG] = m
        lo, hi = m[:, :, 0:HALF], m[:, :, HALF:CH]
        msend[s * KG : (s + 1) * KG] = jnp.where(core == 0, hi, lo)
        mm[s * KG : (s + 1) * KG, 0:CELLS] = jnp.where(core == 0, lo, hi)
        c = remote(msend.at[ks], mm.at[ks, pl.ds(CELLS, CELLS)], msem_s.at[s], msem_r.at[s], partner)
        c.start()
        m_copies.append(c)

    scale = 1.0 / math.sqrt(CELLS * 512)
    own = pl.ds(pl.multiple_of(rank * SLICE, SLICE), SLICE)
    for s in range(GROUPS):
        m_copies[s].wait_recv()
        for k in range(s * KG, (s + 1) * KG):
            part = jnp.dot(gt[...], mm[k], preferred_element_type=F32) * scale
            dws[k] = part.astype(BF16)
        for d in range(1, 16):
            peer_rows = pl.ds(pl.multiple_of(lax.rem(rank + d, 16) * SLICE, SLICE), SLICE)
            remote(
                dws.at[pl.ds(s * KG, KG), peer_rows], rsb.at[s, d - 1], rs_s.at[s], rs_r.at[s], plane_peer(d)
            ).start()

    acc = jnp.zeros((CELLS, CH), F32)
    for k in range(K):
        acc += lax.dot_general(mfull[k], w_ref[k], (((1,), (1,)), ((), ())), preferred_element_type=F32)
    out_ref[...] = acc.astype(BF16).reshape(ROWS, COLS, CH)

    for s in range(GROUPS):
        whole_wait(rsb.at[s], rs_r.at[s])
        part = dws[s * KG : (s + 1) * KG, own, :].astype(F32)
        for d in range(15):
            part += rsb[s, d].astype(F32)
        zs[s] = part.astype(BF16)

        @pl.when(z4 != s)
        def _():
            slot = lax.rem(z4 - s + 4, 4) - 1
            remote(zs.at[s], zb.at[slot], z_s.at[s], z_r, z4_peer(s)).start()

    @pl.when(z4 < GROUPS)
    def _():
        whole_wait(zb, z_r)
        part = zs[z4].astype(F32)
        for d in range(3):
            part += zb[d].astype(F32)
        zg[zgroup] = part.astype(BF16)
        for d in range(1, 4):
            remote(
                zg.at[zgroup], zg.at[zgroup], zg_s, zg_r, zfar_peer(lax.rem(zgroup + d, 4))
            ).start()

    ig_east.wait_recv()
    ig_west.wait_recv()
    total = mid[:, COLS : 2 * COLS] + lon_in[0].astype(F32) + lon_in[1].astype(F32)
    ig_ref[...] = total.astype(BF16)

    @pl.when(z4 < GROUPS)
    def _():
        whole_wait(zgd, zg_r)
        part = zg[0].astype(F32)
        for d in range(1, 4):
            part += zg[d].astype(F32)
        fin[z4] = part.astype(BF16)
        for d in range(1, 4):
            remote(fin.at[z4], fin.at[z4], fin_s, fin_r.at[z4], z4_peer(lax.rem(z4 + d, 4))).start()

    for s in range(GROUPS):
        @pl.when(z4 != s)
        def _():
            whole_wait(fin.at[s], fin_r.at[s])

        ks = pl.ds(s * KG, KG)
        for d in range(1, 16):
            remote(fin.at[s], dwv.at[ks, own], ag_s.at[s], ag_r.at[s], plane_peer(d)).start()
        dwv[s * KG : (s + 1) * KG, own, :] = fin[s]

    half = pl.ds(pl.multiple_of(core * HALF, HALF), HALF)
    tails = []
    for s in range(GROUPS):
        ks = pl.ds(s * KG, KG)
        whole_wait(rsb.at[s], ag_r.at[s])
        c = remote(dwv.at[ks], dw_ref.at[ks, :, half], fw_s.at[s], fw_r.at[s], partner)
        c.start()
        e = pltpu.make_async_copy(dwv.at[ks], dw_ref.at[ks, :, half], loc.at[s])
        e.start()
        tails.append((c, e))

    for s in range(GROUPS):
        whole_wait(rsb.at[s], rs_s.at[s])
        whole_wait(rsb.at[s], ag_s.at[s])

        @pl.when(z4 != s)
        def _():
            whole_wait(zs.at[s], z_s.at[s])

        m_copies[s].wait_send()

    @pl.when(z4 < GROUPS)
    def _():
        whole_wait(zgd, zg_s)
        whole_wait(zgd, fin_s)

    g_send.wait_send()
    to_east.wait_send()
    to_west.wait_send()
    ig_east.wait_send()
    ig_west.wait_send()

    @pl.when(has_up)
    def _():
        for pair in verticals + ((ig_up, ig_down),):
            pair[0].wait_send()

    @pl.when(has_down)
    def _():
        for pair in verticals + ((ig_up, ig_down),):
            pair[1].wait_send()

    for c, e in tails:
        c.wait()
        e.wait()


def on_device(inputs, out_grad, weight, kernel_basis, band_start, band_width, lon_reach):
    vmem = pl.BlockSpec(memory_space=pltpu.VMEM)
    smem = pl.BlockSpec(memory_space=pltpu.SMEM)
    hbm = pl.BlockSpec(memory_space=pl.ANY)
    dma = pltpu.SemaphoreType.DMA
    scratch = [
        pltpu.VMEM((EXT, PITCH, CH), BF16),
        pltpu.VMEM((ROWS, 32, 128), F32),
        pltpu.VMEM((ROWS, 24, 128), F32),
        pltpu.VMEM((K, CELLS, FLAT), BF16),
        pltpu.VMEM((K, CH, CELLS), BF16),
        pltpu.VMEM((CH, K * CELLS), BF16),
        pltpu.VMEM((ROWS, 3 * COLS, CH), F32),
        pltpu.VMEM((2, ROWS, 3 * COLS, CH), BF16),
        pltpu.VMEM((2, ROWS, 3 * COLS, CH), BF16),
        pltpu.VMEM((2, ROWS, COLS, CH), BF16),
        pltpu.VMEM((2, ROWS, COLS, CH), BF16),
        pltpu.VMEM((CH, 2 * CELLS), BF16),
        pltpu.VMEM((ROWS, COLS, CH), BF16),
        pltpu.VMEM((K, CELLS, CH), BF16),
        pltpu.VMEM((K, 2 * CELLS, HALF), BF16),
        pltpu.VMEM((K, CELLS, HALF), BF16),
        pltpu.VMEM((K, CH, HALF), BF16),
        pltpu.VMEM((GROUPS, 15, KG, SLICE, HALF), BF16),
        pltpu.VMEM((GROUPS, KG, SLICE, HALF), BF16),
        pltpu.VMEM((3, KG, SLICE, HALF), BF16),
        pltpu.VMEM((4, KG, SLICE, HALF), BF16),
        pltpu.VMEM((3, KG, SLICE, HALF), BF16),
        pltpu.VMEM((GROUPS, KG, SLICE, HALF), BF16),
        pltpu.VMEM((K, CH, HALF), BF16),
        dma((8,)), dma((8,)), dma((2,)), dma((4,)), dma((4,)), dma((3,)), dma((3,)),
        dma((3,)), dma((3,)), dma((3,)), dma, dma, dma, dma, dma((3,)), dma((3,)), dma((3,)),
        dma((3,)), dma((3,)), dma((3,)),
    ]
    out, ig, dw = pl.pallas_call(
        kernel,
        out_shape=(
            jax.ShapeDtypeStruct((ROWS, COLS, CH), BF16),
            jax.ShapeDtypeStruct((ROWS, COLS, CH), BF16),
            jax.ShapeDtypeStruct((K, CH, CH), BF16),
        ),
        in_specs=[vmem, vmem, vmem, vmem, smem, smem, smem],
        out_specs=(vmem, vmem, hbm),
        scratch_shapes=scratch,
        compiler_params=pltpu.CompilerParams(collective_id=0, has_side_effects=True, vmem_limit_bytes=40 << 20),
    )(inputs, out_grad, weight, kernel_basis, band_start, band_width, lon_reach)
    return out, ig, dw.astype(F32)


def solution(mesh):
    placed = (
        P("lat", "lon", None),
        P("lat", "lon", None),
        P(),
        P("lat", None, None, None),
        P("lat"),
        P("lat"),
        P("lat"),
    )
    return jax.shard_map(
        on_device,
        mesh=mesh,
        in_specs=placed,
        out_specs=(P("lat", "lon", None), P("lat", "lon", None), P()),
        check_vma=False,
    )
```

```python
import functools
import math

import jax
import jax.numpy as jnp
from jax import lax
from jax.experimental import pallas as pl
from jax.experimental.pallas import tpu as pltpu
from jax.sharding import PartitionSpec as P

MESH = pl.DeviceIdType.MESH
F32, BF16 = jnp.float32, jnp.bfloat16

ROWS, COLS, CH = 8, 16, 256
CELLS = ROWS * COLS
K, BAND, LONW = 9, 17, 33
EXT = 3 * ROWS
PITCH = 64
FLAT = EXT * PITCH
PAIRS = EXT // 2
HALF = 128
GROUPS = 3
KG = K // GROUPS
SLICE = 16


def whole_wait(buf, sem):
    pltpu.make_async_copy(buf, buf, sem).wait()


def kernel(
    x_ref, g_ref, w_ref, kb_ref, start_ref, width_ref, reach_ref,
    out_ref, ig_ref, dw_ref,
    start_v, width_v, reach_v, wv, kbv, mask, kbs, comb, op,
    xh, xtc, xc, em, xt, gs, mt, mg, mgt, mid, lat_out, lat_in, lon_out, lon_in, mfull,
    wcs, wcr, zs, zb, zg, zgd, fin, dwv, dwt, eye,
    lsem, xsend, xrecv, xa_s, xa_r, seam_s, seam_r, fsend, frecv, g_s, g_r, igsend, igrecv, wsem,
    z_s, z_r, zg_s, zg_r, fin_s, fin_r, ag_s, ag_r, fw_s, fw_r, loc,
):
    lat, lon = lax.axis_index("lat"), lax.axis_index("lon")
    core = lax.rem(lat, 2)
    zlo = lat // 2
    zhi = lon // 16
    rank = lax.rem(lon, 16)
    z4 = lax.rem(zlo, 4)
    zgroup = zhi * 2 + zlo // 4
    up, down = lat - 1, lat + 1
    has_up, has_down = lat > 0, lat < 15
    east, west = lax.rem(lon + 1, 32), lax.rem(lon + 31, 32)
    partner = (lat + 1 - 2 * core, lon)
    first_sector, last_sector = rank == 0, rank == 15

    def plane_peer(d):
        return (lat, zhi * 16 + lax.rem(rank + d, 16))

    def other_half(t):
        return (lat, (1 - zhi) * 16 + t)

    def z4_peer(t):
        return ((zlo - z4 + t) * 2 + core, lon)

    def zfar_peer(t):
        return (((t % 2) * 4 + z4) * 2 + core, (t // 2) * 16 + rank)

    def remote(src, dst, ssem, rsem, dev):
        return pltpu.make_async_remote_copy(
            src_ref=src, dst_ref=dst, send_sem=ssem, recv_sem=rsem, device_id=dev, device_id_type=MESH
        )

    mid_rows, top, bottom = pl.ds(ROWS, ROWS), pl.ds(0, ROWS), pl.ds(2 * ROWS, ROWS)
    mid_cols, wcols, ecols = pl.ds(COLS, COLS), pl.ds(0, COLS), pl.ds(2 * COLS, COLS)

    local = [
        pltpu.make_async_copy(kb_ref, kbv, lsem.at[0]),
        pltpu.make_async_copy(start_ref, start_v, lsem.at[1]),
        pltpu.make_async_copy(width_ref, width_v, lsem.at[2]),
        pltpu.make_async_copy(reach_ref, reach_v, lsem.at[3]),
        pltpu.make_async_copy(g_ref, gs.at[rank], lsem.at[4]),
        pltpu.make_async_copy(w_ref, wv, lsem.at[5]),
        pltpu.make_async_copy(x_ref, xh.at[mid_rows, mid_cols], lsem.at[6]),
    ]
    for c in local[:-1]:
        c.start()
    xh[...] = jnp.zeros_like(xh)
    local[-1].start()
    xc[...] = jnp.zeros_like(xc)
    lat_in[...] = jnp.zeros_like(lat_in)

    bar = pltpu.get_barrier_semaphore()

    def signal(dev):
        pl.semaphore_signal(bar, inc=1, device_id=dev, device_id_type=MESH)

    signal(other_half(0))
    signal(other_half(15))
    signal((lat, east))
    signal((lat, west))
    for d in range(1, 4):
        signal(zfar_peer(lax.rem(zgroup + d, 4)))
    for d in range(1, 16):
        signal(plane_peer(d))
    for d in range(1, 4):
        signal(z4_peer(lax.rem(z4 + d, 4)))

    @pl.when(has_up)
    def _():
        signal((up, lon))

    @pl.when(has_down)
    def _():
        signal((down, lon))

    kbs[...] = jnp.zeros_like(kbs)
    row = lax.broadcasted_iota(jnp.int32, (ROWS, ROWS), 0)
    eye[...] = (
        lax.broadcasted_iota(jnp.int32, (CH, CH), 0) == lax.broadcasted_iota(jnp.int32, (CH, CH), 1)
    ).astype(F32).astype(BF16)
    cell = lax.broadcasted_iota(jnp.int32, (3 * CELLS, ROWS * PITCH), 0)
    place = (cell % CELLS) // COLS * PITCH + cell // CELLS * COLS + cell % COLS
    em[...] = (place == lax.broadcasted_iota(jnp.int32, (3 * CELLS, ROWS * PITCH), 1)).astype(F32).astype(BF16)

    for c in local[:4]:
        c.wait()
    row = lax.broadcasted_iota(jnp.int32, (BAND, ROWS, LONW), 1)
    band_pos = lax.broadcasted_iota(jnp.int32, (BAND, ROWS, LONW), 0)
    lon_off = jnp.abs(lax.broadcasted_iota(jnp.int32, (BAND, ROWS, LONW), 2) - (LONW - 1) // 2)
    inside = jnp.zeros((BAND, ROWS, LONW), jnp.bool_)
    for i in range(ROWS):
        first = start_v[i]
        keep = (band_pos >= first) & (band_pos < first + width_v[i]) & (lon_off <= reach_v[i])
        inside = inside | (keep & (row == i))
    mask[...] = inside.astype(F32)

    def op_step(k, carry):
        kbs[1 : 1 + BAND, :, 0:LONW] = jnp.where(mask[...] > 0.5, kbv[k].astype(F32), 0.0)
        for t in range(BAND + 1):
            comb[t] = kbs[t] + pltpu.roll(kbs[t + 1], PITCH, 1)
        for i in range(ROWS):
            for q in range(PAIRS):
                t = 2 * q - i + 1
                if 0 <= t <= BAND:
                    line = jnp.broadcast_to(comb[t, i : i + 1, :], (COLS, 128))
                    tile = pltpu.roll(line, 0, 1, stride=1, stride_axis=0)
                    op[k, i * COLS : (i + 1) * COLS, q * 128 : (q + 1) * 128] = tile.astype(BF16)
                else:
                    op[k, i * COLS : (i + 1) * COLS, q * 128 : (q + 1) * 128] = jnp.zeros((COLS, 128), BF16)
        return carry

    lax.fori_loop(0, K, op_step, 0)

    local[6].wait()
    xtc[...] = xh[mid_rows, mid_cols, :].reshape(CELLS, CH).astype(F32).T.astype(BF16)
    own = pl.ds(pl.multiple_of(rank * SLICE, SLICE), SLICE)
    xc[1, 1 + rank] = xtc[own, :]

    at_seam = jnp.logical_or(first_sector, last_sector).astype(jnp.int32)
    pl.semaphore_wait(bar, 23 + has_up.astype(jnp.int32) + has_down.astype(jnp.int32) + 16 * at_seam)

    @pl.when(last_sector)
    def _():
        for t in range(16):
            remote(xtc.at[pl.ds(t * SLICE, SLICE)], xc.at[1, 0], seam_s.at[0], seam_r.at[0], other_half(t)).start()

    @pl.when(first_sector)
    def _():
        for t in range(16):
            remote(xtc.at[pl.ds(t * SLICE, SLICE)], xc.at[1, 17], seam_s.at[1], seam_r.at[1], other_half(t)).start()

    for d in range(1, 16):
        peer_rows = pl.ds(pl.multiple_of(lax.rem(rank + d, 16) * SLICE, SLICE), SLICE)
        remote(xtc.at[peer_rows], xc.at[1, 1 + rank], xa_s, xa_r, plane_peer(d)).start()
    local[4].wait()
    for d in range(1, 16):
        remote(gs.at[rank], gs.at[rank], g_s, g_r, plane_peer(d)).start()

    local[5].wait()
    g = gs[rank]

    for k in range(K):
        part = jnp.dot(g, wv[k], preferred_element_type=F32).astype(BF16)
        part = lax.dot_general(eye[...], part, (((1,), (1,)), ((), ())), preferred_element_type=F32)
        mgt[:, k * CELLS : (k + 1) * CELLS] = part.astype(BF16)

    for n in range(FLAT // 256):
        part = jnp.dot(
            mgt[...], op[:, :, n * 256 : (n + 1) * 256].reshape(K * CELLS, 256), preferred_element_type=F32
        )
        part = part.T.reshape(4, PITCH, CH)[:, : 3 * COLS]
        r = n * 4
        if r < ROWS:
            lat_out[0, r : r + 4] = part.astype(BF16)
        elif r < 2 * ROWS:
            mid[r - ROWS : r - ROWS + 4] = part
        else:
            lat_out[1, r - 2 * ROWS : r - 2 * ROWS + 4] = part.astype(BF16)

    def start_vertical(pair):
        @pl.when(has_up)
        def _():
            pair[0].start()

        @pl.when(has_down)
        def _():
            pair[1].start()

    def wait_vertical(pair):
        @pl.when(has_down)
        def _():
            pair[0].wait_recv()

        @pl.when(has_up)
        def _():
            pair[1].wait_recv()

    def forward(slots, s):
        src = xc.at[1, slots]
        return (
            remote(src, xc.at[2, slots], fsend.at[s], frecv.at[s], (up, lon)),
            remote(src, xc.at[0, slots], fsend.at[s + 1], frecv.at[s + 1], (down, lon)),
        )

    forwards = (forward(pl.ds(1, 16), 0), forward(pl.ds(0, 1), 2), forward(pl.ds(17, 1), 4))
    whole_wait(xc.at[1, pl.ds(1, 15)], xa_r)
    start_vertical(forwards[0])
    ig_up = remote(lat_out.at[0], lat_in.at[1], igsend.at[0], igrecv.at[0], (up, lon))
    ig_down = remote(lat_out.at[1], lat_in.at[0], igsend.at[1], igrecv.at[1], (down, lon))
    start_vertical((ig_up, ig_down))

    to_east = remote(x_ref, xh.at[mid_rows, wcols], xsend.at[0], xrecv.at[0], (lat, east))
    to_west = remote(x_ref, xh.at[mid_rows, ecols], xsend.at[1], xrecv.at[1], (lat, west))
    to_east.start()
    to_west.start()

    def up_down(cols, s):
        src = xh.at[mid_rows, cols]
        return (
            remote(src, xh.at[bottom, cols], xsend.at[s], xrecv.at[s], (up, lon)),
            remote(src, xh.at[top, cols], xsend.at[s + 1], xrecv.at[s + 1], (down, lon)),
        )

    verticals = (up_down(mid_cols, 2), up_down(wcols, 4), up_down(ecols, 6))
    start_vertical(verticals[0])

    for s in range(2):
        whole_wait(xc.at[1, 0], seam_r.at[s])
        start_vertical(forwards[1 + s])

    for pair in forwards:
        wait_vertical(pair)
    whole_wait(gs.at[pl.ds(0, 15)], g_r)

    for b in range(3):
        part = jnp.zeros((CH, ROWS * PITCH), F32)
        for d in range(3):
            part += jnp.dot(
                xc[b, d : d + 16].reshape(CH, CELLS), em[d * CELLS : (d + 1) * CELLS], preferred_element_type=F32
            )
        xt[:, b * ROWS * PITCH : (b + 1) * ROWS * PITCH] = part.astype(BF16)
    for s in range(GROUPS):
        part = lax.dot_general(
            xt[...], op[s * KG : (s + 1) * KG].reshape(KG * CELLS, FLAT), (((1,), (1,)), ((), ())),
            preferred_element_type=F32,
        ).astype(BF16)
        for k in range(KG):
            for t in range(16):
                mt[s * KG + k, :, t * CELLS : (t + 1) * CELLS] = part[
                    t * SLICE : (t + 1) * SLICE, k * CELLS : (k + 1) * CELLS
                ]
    scale = 1.0 / math.sqrt(CELLS * 512)
    dwp = jnp.dot(
        mt[...].reshape(K * SLICE, 16 * CELLS), gs[...].reshape(16 * CELLS, CH), preferred_element_type=F32
    )
    dwp = (dwp * scale).reshape(K, SLICE, CH)

    wcs[...] = jnp.where(core == 0, dwp[:, :, HALF:CH], dwp[:, :, 0:HALF])
    w_copy = remote(wcs, wcr, wsem.at[0], wsem.at[1], partner)
    w_copy.start()
    keep_half = jnp.where(core == 0, dwp[:, :, 0:HALF], dwp[:, :, HALF:CH])
    w_copy.wait_recv()
    keep_half = keep_half + wcr[...]

    for s in range(GROUPS):
        zs[s] = keep_half[s * KG : (s + 1) * KG].astype(BF16)

        @pl.when(z4 != s)
        def _():
            slot = lax.rem(z4 - s + 4, 4) - 1
            remote(zs.at[s], zb.at[slot], z_s.at[s], z_r, z4_peer(s)).start()

    wait_vertical((ig_up, ig_down))
    total = mid[...] + lat_in[0].astype(F32) + lat_in[1].astype(F32)
    lon_out[0] = total[:, 0:COLS].astype(BF16)
    lon_out[1] = total[:, 2 * COLS : 3 * COLS].astype(BF16)
    mid[:, COLS : 2 * COLS] = total[:, COLS : 2 * COLS]
    ig_west = remote(lon_out.at[0], lon_in.at[1], igsend.at[2], igrecv.at[2], (lat, west))
    ig_east = remote(lon_out.at[1], lon_in.at[0], igsend.at[3], igrecv.at[3], (lat, east))
    ig_west.start()
    ig_east.start()

    @pl.when(z4 < GROUPS)
    def _():
        whole_wait(zb, z_r)
        part = zs[z4].astype(F32)
        for d in range(3):
            part += zb[d].astype(F32)
        zg[zgroup] = part.astype(BF16)
        for d in range(1, 4):
            remote(
                zg.at[zgroup], zg.at[zgroup], zg_s, zg_r, zfar_peer(lax.rem(zgroup + d, 4))
            ).start()

    to_east.wait_recv()
    start_vertical(verticals[1])
    to_west.wait_recv()
    start_vertical(verticals[2])
    for pair in verticals:
        wait_vertical(pair)

    flat_x = xh[...].reshape(FLAT, CH)
    acc = jnp.zeros((CELLS, CH), F32)
    for s in range(GROUPS):
        m = jnp.dot(op[s * KG : (s + 1) * KG].reshape(KG * CELLS, FLAT), flat_x, preferred_element_type=F32)
        m = m.astype(BF16).reshape(KG, CELLS, CH)
        for k in range(KG):
            acc += lax.dot_general(m[k], wv[s * KG + k], (((1,), (1,)), ((), ())), preferred_element_type=F32)
    out_ref[...] = acc.astype(BF16).reshape(ROWS, COLS, CH)

    @pl.when(z4 < GROUPS)
    def _():
        whole_wait(zgd, zg_r)
        part = zg[0].astype(F32)
        for d in range(1, 4):
            part += zg[d].astype(F32)
        fin[z4] = part.astype(BF16)
        for d in range(1, 4):
            remote(fin.at[z4], fin.at[z4], fin_s, fin_r.at[z4], z4_peer(lax.rem(z4 + d, 4))).start()

    for s in range(GROUPS):
        @pl.when(z4 != s)
        def _():
            whole_wait(fin.at[s], fin_r.at[s])

        ks = pl.ds(s * KG, KG)
        for d in range(1, 16):
            remote(fin.at[s], dwv.at[ks, own], ag_s.at[s], ag_r.at[s], plane_peer(d)).start()
        dwv[s * KG : (s + 1) * KG, own, :] = fin[s]

    ig_east.wait_recv()
    ig_west.wait_recv()
    total = mid[:, COLS : 2 * COLS] + lon_in[0].astype(F32) + lon_in[1].astype(F32)
    ig_ref[...] = total.astype(BF16)

    half = pl.ds(pl.multiple_of(core * HALF, HALF), HALF)
    small_eye = eye[0:HALF, 0:HALF]
    tails = []
    for s in range(GROUPS):
        ks = pl.ds(s * KG, KG)
        whole_wait(dwv.at[ks, pl.ds(0, 15 * SLICE)], ag_r.at[s])
        for k in range(s * KG, (s + 1) * KG):
            part = lax.dot_general(small_eye, dwv[k], (((1,), (1,)), ((), ())), preferred_element_type=F32)
            dwt[k] = part.astype(BF16)
        c = remote(dwt.at[ks], dw_ref.at[ks, half], fw_s.at[s], fw_r.at[s], partner)
        c.start()
        e = pltpu.make_async_copy(dwt.at[ks], dw_ref.at[ks, half], loc.at[s])
        e.start()
        tails.append((c, e))

    for s in range(GROUPS):
        whole_wait(dwv.at[pl.ds(s * KG, KG), pl.ds(0, 15 * SLICE)], ag_s.at[s])

        @pl.when(z4 != s)
        def _():
            whole_wait(zs.at[s], z_s.at[s])

    @pl.when(z4 < GROUPS)
    def _():
        whole_wait(zgd, zg_s)
        whole_wait(zgd, fin_s)

    @pl.when(last_sector)
    def _():
        whole_wait(xtc, seam_s.at[0])

    @pl.when(first_sector)
    def _():
        whole_wait(xtc, seam_s.at[1])

    whole_wait(xc.at[1, pl.ds(1, 15)], xa_s)
    whole_wait(gs.at[pl.ds(0, 15)], g_s)
    w_copy.wait_send()
    to_east.wait_send()
    to_west.wait_send()
    ig_east.wait_send()
    ig_west.wait_send()

    @pl.when(has_up)
    def _():
        for pair in verticals + forwards + ((ig_up, ig_down),):
            pair[0].wait_send()

    @pl.when(has_down)
    def _():
        for pair in verticals + forwards + ((ig_up, ig_down),):
            pair[1].wait_send()

    for c, e in tails:
        c.wait()
        e.wait()


def on_device(inputs, out_grad, weight, kernel_basis, band_start, band_width, lon_reach):
    vmem = pl.BlockSpec(memory_space=pltpu.VMEM)
    hbm = pl.BlockSpec(memory_space=pl.ANY)
    dma = pltpu.SemaphoreType.DMA
    piece = (KG, SLICE, HALF)
    scratch = [
        pltpu.SMEM((ROWS,), jnp.int32),
        pltpu.SMEM((ROWS,), jnp.int32),
        pltpu.SMEM((ROWS,), jnp.int32),
        pltpu.VMEM((K, CH, CH), BF16),
        pltpu.VMEM((K, BAND, ROWS, LONW), BF16),
        pltpu.VMEM((BAND, ROWS, LONW), F32),
        pltpu.VMEM((BAND + 2, ROWS, 128), F32),
        pltpu.VMEM((BAND + 1, ROWS, 128), F32),
        pltpu.VMEM((K, CELLS, FLAT), BF16),
        pltpu.VMEM((EXT, PITCH, CH), BF16),
        pltpu.VMEM((CH, CELLS), BF16),
        pltpu.VMEM((3, 18, SLICE, CELLS), BF16),
        pltpu.VMEM((3 * CELLS, ROWS * PITCH), BF16),
        pltpu.VMEM((CH, FLAT), BF16),
        pltpu.VMEM((16, CELLS, CH), BF16),
        pltpu.VMEM((K, SLICE, 16 * CELLS), BF16),
        pltpu.VMEM((K, CH, CELLS), BF16),
        pltpu.VMEM((CH, K * CELLS), BF16),
        pltpu.VMEM((ROWS, 3 * COLS, CH), F32),
        pltpu.VMEM((2, ROWS, 3 * COLS, CH), BF16),
        pltpu.VMEM((2, ROWS, 3 * COLS, CH), BF16),
        pltpu.VMEM((2, ROWS, COLS, CH), BF16),
        pltpu.VMEM((2, ROWS, COLS, CH), BF16),
        pltpu.VMEM((K, CELLS, CH), BF16),
        pltpu.VMEM((K, SLICE, HALF), F32),
        pltpu.VMEM((K, SLICE, HALF), F32),
        pltpu.VMEM((GROUPS,) + piece, BF16),
        pltpu.VMEM((3,) + piece, BF16),
        pltpu.VMEM((4,) + piece, BF16),
        pltpu.VMEM((3,) + piece, BF16),
        pltpu.VMEM((GROUPS,) + piece, BF16),
        pltpu.VMEM((K, CH, HALF), BF16),
        pltpu.VMEM((K, HALF, CH), BF16),
        pltpu.VMEM((CH, CH), BF16),
        dma((7,)), dma((8,)), dma((8,)), dma, dma, dma((2,)), dma((2,)), dma((6,)), dma((6,)), dma, dma,
        dma((4,)), dma((4,)), dma((2,)),
        dma((3,)), dma, dma, dma, dma, dma((3,)), dma((3,)), dma((3,)), dma((3,)), dma((3,)), dma((3,)),
    ]
    out, ig, dw = pl.pallas_call(
        kernel,
        out_shape=(
            jax.ShapeDtypeStruct((ROWS, COLS, CH), BF16),
            jax.ShapeDtypeStruct((ROWS, COLS, CH), BF16),
            jax.ShapeDtypeStruct((K, CH, CH), BF16),
        ),
        in_specs=[hbm] * 7,
        out_specs=(vmem, vmem, hbm),
        scratch_shapes=scratch,
        compiler_params=pltpu.CompilerParams(collective_id=0, has_side_effects=True, vmem_limit_bytes=56 << 20),
    )(
        inputs, out_grad.reshape(CELLS, CH), weight, kernel_basis.transpose(1, 2, 0, 3),
        band_start, band_width, lon_reach,
    )
    return out, ig, dw.astype(F32)


def solution(mesh):
    placed = (
        P("lat", "lon", None),
        P("lat", "lon", None),
        P(),
        P("lat", None, None, None),
        P("lat"),
        P("lat"),
        P("lat"),
    )
    return jax.shard_map(
        on_device,
        mesh=mesh,
        in_specs=placed,
        out_specs=(P("lat", "lon", None), P("lat", "lon", None), P()),
        check_vma=False,
    )
```

```python
import functools
import math

import jax
import jax.numpy as jnp
from jax import lax
from jax.experimental import pallas as pl
from jax.experimental.pallas import tpu as pltpu
from jax.sharding import PartitionSpec as P

MESH = pl.DeviceIdType.MESH
F32, BF16 = jnp.float32, jnp.bfloat16

ROWS, COLS, CH = 8, 16, 256
CELLS = ROWS * COLS
K, BAND, LONW = 9, 17, 33
EXT = 3 * ROWS
PITCH = 64
FLAT = EXT * PITCH
PAIRS = EXT // 2
HALF = 128
GROUPS = 3
KG = K // GROUPS
SLICE = 16


def whole_wait(buf, sem):
    pltpu.make_async_copy(buf, buf, sem).wait()


def kernel(
    x_ref, g_ref, w_ref, kb_ref, start_ref, width_ref, reach_ref,
    out_ref, ig_ref, dw_ref,
    start_v, width_v, reach_v, wv, kbv, mask, kbs, comb, op,
    xh, xtc, xc, em, xt, gs, mt, mgt, mid, lat_out, lat_in, lon_out, lon_in, dwp,
    wcs, wcr, zs, zb, zg, zgd, fin, dwv, sg, eye,
    lsem, xsend, xrecv, xa_s, xa_r, seam_s, seam_r, fsend, frecv, g_s, g_r, igsend, igrecv, wsem,
    z_s, z_r, zg_s, zg_r, fin_s, fin_r, ag_s, ag_r, fw_s, fw_r, sg_s, sg_r,
):
    lat, lon = lax.axis_index("lat"), lax.axis_index("lon")
    core = lax.rem(lat, 2)
    zlo = lat // 2
    zhi = lon // 16
    rank = lax.rem(lon, 16)
    z4 = lax.rem(zlo, 4)
    zgroup = zhi * 2 + zlo // 4
    up, down = lat - 1, lat + 1
    has_up, has_down = lat > 0, lat < 15
    east, west = lax.rem(lon + 1, 32), lax.rem(lon + 31, 32)
    partner = (lat + 1 - 2 * core, lon)
    not_first, not_last = rank > 0, rank < 15

    def plane_peer(d):
        return (lat, zhi * 16 + lax.rem(rank + d, 16))

    other_half = (lat, (1 - zhi) * 16 + rank)

    def z4_peer(t):
        return ((zlo - z4 + t) * 2 + core, lon)

    def zfar_peer(t):
        return (((t % 2) * 4 + z4) * 2 + core, (t // 2) * 16 + rank)

    def remote(src, dst, ssem, rsem, dev):
        return pltpu.make_async_remote_copy(
            src_ref=src, dst_ref=dst, send_sem=ssem, recv_sem=rsem, device_id=dev, device_id_type=MESH
        )

    mid_rows, top, bottom = pl.ds(ROWS, ROWS), pl.ds(0, ROWS), pl.ds(2 * ROWS, ROWS)
    mid_cols, wcols, ecols = pl.ds(COLS, COLS), pl.ds(0, COLS), pl.ds(2 * COLS, COLS)

    local = [
        pltpu.make_async_copy(kb_ref, kbv, lsem.at[0]),
        pltpu.make_async_copy(start_ref, start_v, lsem.at[1]),
        pltpu.make_async_copy(width_ref, width_v, lsem.at[2]),
        pltpu.make_async_copy(reach_ref, reach_v, lsem.at[3]),
        pltpu.make_async_copy(g_ref, gs.at[rank], lsem.at[4]),
        pltpu.make_async_copy(w_ref, wv, lsem.at[5]),
        pltpu.make_async_copy(x_ref, xh.at[mid_rows, mid_cols], lsem.at[6]),
    ]
    for c in (local[6],) + tuple(local[:6]):
        c.start()

    @pl.when(jnp.logical_not(has_up))
    def _():
        xh[0:ROWS] = jnp.zeros((ROWS, PITCH, CH), BF16)
        xc[0] = jnp.zeros((18, SLICE, CELLS), BF16)
        lat_in[0] = jnp.zeros((ROWS, 3 * COLS, CH), BF16)

    @pl.when(jnp.logical_not(has_down))
    def _():
        xh[2 * ROWS : EXT] = jnp.zeros((ROWS, PITCH, CH), BF16)
        xc[2] = jnp.zeros((18, SLICE, CELLS), BF16)
        lat_in[1] = jnp.zeros((ROWS, 3 * COLS, CH), BF16)

    bar = pltpu.get_barrier_semaphore()

    def signal(dev):
        pl.semaphore_signal(bar, inc=1, device_id=dev, device_id_type=MESH)

    for d in range(1, 4):
        signal(zfar_peer(lax.rem(zgroup + d, 4)))
    for d in range(1, 16):
        signal(plane_peer(d))
    for d in range(1, 4):
        signal(z4_peer(lax.rem(z4 + d, 4)))

    @pl.when(has_up)
    def _():
        signal((up, lon))

    @pl.when(has_down)
    def _():
        signal((down, lon))

    local[6].wait()
    xtc[...] = xh[mid_rows, mid_cols, :].reshape(CELLS, CH).astype(F32).T.astype(BF16)
    own = pl.ds(pl.multiple_of(rank * SLICE, SLICE), SLICE)
    xc[1, 1 + rank] = xtc[own, :]

    kbs[...] = jnp.zeros_like(kbs)
    xh[:, 3 * COLS : PITCH] = jnp.zeros((EXT, PITCH - 3 * COLS, CH), BF16)
    eye[...] = (
        lax.broadcasted_iota(jnp.int32, (CH, CH), 0) == lax.broadcasted_iota(jnp.int32, (CH, CH), 1)
    ).astype(F32).astype(BF16)
    cell = lax.broadcasted_iota(jnp.int32, (3 * CELLS, ROWS * PITCH), 0)
    place = (cell % CELLS) // COLS * PITCH + cell // CELLS * COLS + cell % COLS
    em[...] = (place == lax.broadcasted_iota(jnp.int32, (3 * CELLS, ROWS * PITCH), 1)).astype(F32).astype(BF16)

    for c in local[:4]:
        c.wait()
    row = lax.broadcasted_iota(jnp.int32, (BAND, ROWS, LONW), 1)
    band_pos = lax.broadcasted_iota(jnp.int32, (BAND, ROWS, LONW), 0)
    lon_off = jnp.abs(lax.broadcasted_iota(jnp.int32, (BAND, ROWS, LONW), 2) - (LONW - 1) // 2)
    inside = jnp.zeros((BAND, ROWS, LONW), jnp.bool_)
    for i in range(ROWS):
        first = start_v[i]
        keep = (band_pos >= first) & (band_pos < first + width_v[i]) & (lon_off <= reach_v[i])
        inside = inside | (keep & (row == i))
    mask[...] = inside.astype(F32)

    def op_step(k, carry):
        kbs[1 : 1 + BAND, :, 0:LONW] = jnp.where(mask[...] > 0.5, kbv[k].astype(F32), 0.0)
        for t in range(BAND + 1):
            comb[t] = kbs[t] + pltpu.roll(kbs[t + 1], PITCH, 1)
        for i in range(ROWS):
            for q in range(PAIRS):
                t = 2 * q - i + 1
                if 0 <= t <= BAND:
                    line = jnp.broadcast_to(comb[t, i : i + 1, :], (COLS, 128))
                    tile = pltpu.roll(line, 0, 1, stride=1, stride_axis=0)
                    op[k, i * COLS : (i + 1) * COLS, q * 128 : (q + 1) * 128] = tile.astype(BF16)
                else:
                    op[k, i * COLS : (i + 1) * COLS, q * 128 : (q + 1) * 128] = jnp.zeros((COLS, 128), BF16)
        return carry

    lax.fori_loop(0, K, op_step, 0)

    pl.semaphore_wait(bar, 21 + has_up.astype(jnp.int32) + has_down.astype(jnp.int32))

    for d in range(1, 16):
        peer_rows = pl.ds(pl.multiple_of(lax.rem(rank + d, 16) * SLICE, SLICE), SLICE)
        remote(xtc.at[peer_rows], xc.at[1, 1 + rank], xa_s, xa_r, plane_peer(d)).start()
    local[4].wait()
    for d in range(1, 16):
        remote(gs.at[rank], gs.at[rank], g_s, g_r, plane_peer(d)).start()


    def start_vertical(pair):
        @pl.when(has_up)
        def _():
            pair[0].start()

        @pl.when(has_down)
        def _():
            pair[1].start()

    def wait_vertical(pair):
        @pl.when(has_down)
        def _():
            pair[0].wait_recv()

        @pl.when(has_up)
        def _():
            pair[1].wait_recv()

    def forward(slots, s):
        src = xc.at[1, slots]
        return (
            remote(src, xc.at[2, slots], fsend.at[s], frecv.at[s], (up, lon)),
            remote(src, xc.at[0, slots], fsend.at[s + 1], frecv.at[s + 1], (down, lon)),
        )

    forwards = (forward(pl.ds(1, 16), 0), forward(pl.ds(0, 1), 2), forward(pl.ds(17, 1), 4))
    whole_wait(xc.at[1, pl.ds(1, 15)], xa_r)
    seams = (
        remote(xc.at[1, 16], xc.at[1, 0], seam_s.at[0], seam_r.at[0], other_half),
        remote(xc.at[1, 1], xc.at[1, 17], seam_s.at[1], seam_r.at[1], other_half),
    )
    for c in seams:
        c.start()
    start_vertical(forwards[0])

    to_east = remote(x_ref, xh.at[mid_rows, wcols], xsend.at[0], xrecv.at[0], (lat, east))
    to_west = remote(x_ref, xh.at[mid_rows, ecols], xsend.at[1], xrecv.at[1], (lat, west))

    @pl.when(not_last)
    def _():
        to_east.start()

    @pl.when(not_first)
    def _():
        to_west.start()

    local[5].wait()
    g = gs[rank]

    for k in range(K):
        part = jnp.dot(g, wv[k], preferred_element_type=F32).astype(BF16)
        part = lax.dot_general(eye[...], part, (((1,), (1,)), ((), ())), preferred_element_type=F32)
        mgt[:, k * CELLS : (k + 1) * CELLS] = part.astype(BF16)

    for n in range(FLAT // 256):
        part = jnp.dot(
            mgt[...], op[:, :, n * 256 : (n + 1) * 256].reshape(K * CELLS, 256), preferred_element_type=F32
        )
        part = part.T.reshape(4, PITCH, CH)[:, : 3 * COLS]
        r = n * 4
        if r < ROWS:
            lat_out[0, r : r + 4] = part.astype(BF16)
        elif r < 2 * ROWS:
            mid[r - ROWS : r - ROWS + 4] = part
        else:
            lat_out[1, r - 2 * ROWS : r - 2 * ROWS + 4] = part.astype(BF16)

    ig_up = remote(lat_out.at[0], lat_in.at[1], igsend.at[0], igrecv.at[0], (up, lon))
    ig_down = remote(lat_out.at[1], lat_in.at[0], igsend.at[1], igrecv.at[1], (down, lon))
    start_vertical((ig_up, ig_down))

    def up_down(cols, s):
        src = xh.at[mid_rows, cols]
        return (
            remote(src, xh.at[bottom, cols], xsend.at[s], xrecv.at[s], (up, lon)),
            remote(src, xh.at[top, cols], xsend.at[s + 1], xrecv.at[s + 1], (down, lon)),
        )

    verticals = (up_down(mid_cols, 2), up_down(wcols, 4), up_down(ecols, 6))
    start_vertical(verticals[0])

    def windows(slots):
        blocks = []
        for b in range(3):
            part = None
            for d in range(3):
                rows = [xc[b, a + d : a + d + n] for a, n in slots]
                rows = rows[0] if len(rows) == 1 else jnp.concatenate(rows, axis=0)
                term = jnp.dot(
                    rows.reshape(rows.shape[0] * SLICE, CELLS), em[d * CELLS : (d + 1) * CELLS],
                    preferred_element_type=F32,
                )
                part = term if part is None else part + term
            blocks.append(part.astype(BF16))
        return blocks

    def mixed(x, sectors):
        for s in range(GROUPS):
            part = lax.dot_general(
                x, op[s * KG : (s + 1) * KG].reshape(KG * CELLS, FLAT), (((1,), (1,)), ((), ())),
                preferred_element_type=F32,
            ).astype(BF16)
            for k in range(KG):
                for n, t in enumerate(sectors):
                    mt[s * KG + k, :, t * CELLS : (t + 1) * CELLS] = part[
                        n * SLICE : (n + 1) * SLICE, k * CELLS : (k + 1) * CELLS
                    ]

    def grad_term(a, n):
        return jnp.dot(
            mt[:, :, a * CELLS : (a + n) * CELLS].reshape(K * SLICE, n * CELLS), gs[a : a + n].reshape(n * CELLS, CH),
            preferred_element_type=F32,
        )

    wait_vertical(forwards[0])
    for b, block in enumerate(windows(((1, 14),))):
        xt[:, b * ROWS * PITCH : (b + 1) * ROWS * PITCH] = block
    mixed(xt[...], range(1, 15))
    whole_wait(gs.at[pl.ds(0, 15)], g_r)
    dwp[...] = grad_term(1, 14)

    wait_vertical((ig_up, ig_down))
    total = mid[...] + lat_in[0].astype(F32) + lat_in[1].astype(F32)
    lon_out[0] = total[:, 0:COLS].astype(BF16)
    lon_out[1] = total[:, 2 * COLS : 3 * COLS].astype(BF16)
    mid[:, COLS : 2 * COLS] = total[:, COLS : 2 * COLS]
    ig_west = remote(lon_out.at[0], lon_in.at[1], igsend.at[2], igrecv.at[2], (lat, west))
    ig_east = remote(lon_out.at[1], lon_in.at[0], igsend.at[3], igrecv.at[3], (lat, east))
    for s in range(2):
        seams[s].wait_recv()
        start_vertical(forwards[1 + s])
    for pair in forwards[1:]:
        wait_vertical(pair)
    for b, block in enumerate(windows(((0, 1), (15, 1)))):
        xt[0 : 2 * SLICE, b * ROWS * PITCH : (b + 1) * ROWS * PITCH] = block
    mixed(xt[0 : 2 * SLICE, :], (0, 15))
    scale = 1.0 / math.sqrt(CELLS * 512)
    term = (dwp[...] + grad_term(0, 1) + grad_term(15, 1)) * scale
    term = term.reshape(K, SLICE, CH)

    wcs[...] = jnp.where(core == 0, term[:, :, HALF:CH], term[:, :, 0:HALF])
    w_copy = remote(wcs, wcr, wsem.at[0], wsem.at[1], partner)
    w_copy.start()
    keep_half = jnp.where(core == 0, term[:, :, 0:HALF], term[:, :, HALF:CH])
    w_copy.wait_recv()
    keep_half = keep_half + wcr[...]

    for s in range(GROUPS):
        zs[s] = keep_half[s * KG : (s + 1) * KG].astype(BF16)

        @pl.when(z4 != s)
        def _():
            slot = lax.rem(z4 - s + 4, 4) - 1
            remote(zs.at[s], zb.at[slot], z_s.at[s], z_r, z4_peer(s)).start()

    ig_west.start()
    ig_east.start()

    to_first = remote(xc.at[:, 0], sg.at[rank], sg_s.at[0], sg_r, (lat, zhi * 16))
    to_last = remote(xc.at[:, 17], sg.at[rank], sg_s.at[1], sg_r, (lat, zhi * 16 + 15))

    @pl.when(not_first)
    def _():
        to_first.start()
        to_east.wait_recv()
        start_vertical(verticals[1])

    @pl.when(not_last)
    def _():
        to_last.start()
        to_west.wait_recv()
        start_vertical(verticals[2])

    @pl.when(z4 < GROUPS)
    def _():
        whole_wait(zb, z_r)
        part = zs[z4].astype(F32)
        for d in range(3):
            part += zb[d].astype(F32)
        zg[zgroup] = part.astype(BF16)
        for d in range(1, 4):
            remote(
                zg.at[zgroup], zg.at[zgroup], zg_s, zg_r, zfar_peer(lax.rem(zgroup + d, 4))
            ).start()

    @pl.when(z4 < GROUPS)
    def _():
        whole_wait(zgd, zg_r)
        part = zg[0].astype(F32)
        for d in range(1, 4):
            part += zg[d].astype(F32)
        mine = pl.ds(z4 * KG, KG)
        fin[mine] = part.astype(BF16)
        for d in range(1, 4):
            remote(fin.at[mine], fin.at[mine], fin_s, fin_r.at[z4], z4_peer(lax.rem(z4 + d, 4))).start()

    parts = (pl.ds(0, 2 * KG), pl.ds(2 * KG, KG))
    for s in range(GROUPS):
        @pl.when(z4 != s)
        def _():
            whole_wait(fin.at[pl.ds(s * KG, KG)], fin_r.at[s])

        if s == 0:
            continue
        ks = parts[s - 1]
        for d in range(1, 16):
            remote(fin.at[ks], dwv.at[rank, ks], ag_s.at[s - 1], ag_r.at[s - 1], plane_peer(d)).start()
        dwv[rank, ks] = fin[ks]

    wait_vertical(verticals[0])

    def from_sectors(slot, cols):
        whole_wait(sg.at[pl.ds(0, 15)], sg_r)
        sg[rank] = xc[:, slot]
        for b in range(3):
            block = sg[:, b].reshape(CH, CELLS).astype(F32).T.astype(BF16)
            xh[b * ROWS : (b + 1) * ROWS, cols, :] = block.reshape(ROWS, COLS, CH)

    @pl.when(not_first)
    def _():
        wait_vertical(verticals[1])

    @pl.when(not_last)
    def _():
        wait_vertical(verticals[2])

    @pl.when(rank == 0)
    def _():
        from_sectors(0, wcols)

    @pl.when(rank == 15)
    def _():
        from_sectors(17, ecols)

    flat_x = xh[...].reshape(FLAT, CH)
    acc = jnp.zeros((CELLS, CH), F32)
    for s in range(GROUPS):
        m = jnp.dot(op[s * KG : (s + 1) * KG].reshape(KG * CELLS, FLAT), flat_x, preferred_element_type=F32)
        m = m.astype(BF16).reshape(KG, CELLS, CH)
        for k in range(KG):
            acc += lax.dot_general(m[k], wv[s * KG + k], (((1,), (1,)), ((), ())), preferred_element_type=F32)
    out_ref[...] = acc.astype(BF16).reshape(ROWS, COLS, CH)

    ig_east.wait_recv()
    ig_west.wait_recv()
    total = mid[:, COLS : 2 * COLS] + lon_in[0].astype(F32) + lon_in[1].astype(F32)
    ig_ref[...] = total.astype(BF16)

    half = pl.ds(pl.multiple_of(core * HALF, HALF), HALF)
    small_eye = eye[0:HALF, 0:HALF]
    tails = []
    for s, ks in enumerate(parts):
        whole_wait(dwv.at[pl.ds(0, 15), ks], ag_r.at[s])
        for k in range(ks.start, ks.start + ks.size):
            block = dwv[:, k].reshape(CH, HALF)
            part = lax.dot_general(small_eye, block, (((1,), (1,)), ((), ())), preferred_element_type=F32)
            dw_ref[k, half, :] = part.astype(BF16)
        c = remote(dw_ref.at[ks, half], dw_ref.at[ks, half], fw_s.at[s], fw_r.at[s], partner)
        c.start()
        tails.append(c)

    for s, ks in enumerate(parts):
        whole_wait(dwv.at[pl.ds(0, 15), ks], ag_s.at[s])

    for s in range(GROUPS):
        @pl.when(z4 != s)
        def _():
            whole_wait(zs.at[s], z_s.at[s])

    @pl.when(z4 < GROUPS)
    def _():
        whole_wait(zgd, zg_s)
        whole_wait(zgd, fin_s)

    whole_wait(xc.at[1, pl.ds(1, 15)], xa_s)
    whole_wait(gs.at[pl.ds(0, 15)], g_s)
    w_copy.wait_send()
    ig_east.wait_send()
    ig_west.wait_send()

    for c in seams:
        c.wait_send()

    def sent_vertical(pairs):
        @pl.when(has_up)
        def _():
            for pair in pairs:
                pair[0].wait_send()

        @pl.when(has_down)
        def _():
            for pair in pairs:
                pair[1].wait_send()

    sent_vertical(forwards + ((ig_up, ig_down), verticals[0]))

    @pl.when(not_first)
    def _():
        to_first.wait_send()
        to_west.wait_send()
        sent_vertical(verticals[1:2])

    @pl.when(not_last)
    def _():
        to_last.wait_send()
        to_east.wait_send()
        sent_vertical(verticals[2:3])

    for c in tails:
        c.wait()


def finish(out_ref, ig_ref, dw_ref, out_hbm, ig_hbm, dw_hbm, wide, sems):
    copies = [
        pltpu.make_async_copy(out_ref, out_hbm, sems.at[0]),
        pltpu.make_async_copy(ig_ref, ig_hbm, sems.at[1]),
    ]
    for c in copies:
        c.start()
    for k in range(K):
        wide[k] = dw_ref[k].astype(F32)
        c = pltpu.make_async_copy(wide.at[k], dw_hbm.at[k], sems.at[2 + k])
        c.start()
        copies.append(c)
    for c in copies:
        c.wait()


def on_device(inputs, out_grad, weight, kernel_basis, band_start, band_width, lon_reach):
    vmem = pl.BlockSpec(memory_space=pltpu.VMEM)
    hbm = pl.BlockSpec(memory_space=pltpu.HBM)
    dma = pltpu.SemaphoreType.DMA
    piece = (KG, SLICE, HALF)
    scratch = [
        pltpu.SMEM((ROWS,), jnp.int32),
        pltpu.SMEM((ROWS,), jnp.int32),
        pltpu.SMEM((ROWS,), jnp.int32),
        pltpu.VMEM((K, CH, CH), BF16),
        pltpu.VMEM((K, BAND, ROWS, LONW), BF16),
        pltpu.VMEM((BAND, ROWS, LONW), F32),
        pltpu.VMEM((BAND + 2, ROWS, 128), F32),
        pltpu.VMEM((BAND + 1, ROWS, 128), F32),
        pltpu.VMEM((K, CELLS, FLAT), BF16),
        pltpu.VMEM((EXT, PITCH, CH), BF16),
        pltpu.VMEM((CH, CELLS), BF16),
        pltpu.VMEM((3, 18, SLICE, CELLS), BF16),
        pltpu.VMEM((3 * CELLS, ROWS * PITCH), BF16),
        pltpu.VMEM((14 * SLICE, FLAT), BF16),
        pltpu.VMEM((16, CELLS, CH), BF16),
        pltpu.VMEM((K, SLICE, 16 * CELLS), BF16),
        pltpu.VMEM((CH, K * CELLS), BF16),
        pltpu.VMEM((ROWS, 3 * COLS, CH), F32),
        pltpu.VMEM((2, ROWS, 3 * COLS, CH), BF16),
        pltpu.VMEM((2, ROWS, 3 * COLS, CH), BF16),
        pltpu.VMEM((2, ROWS, COLS, CH), BF16),
        pltpu.VMEM((2, ROWS, COLS, CH), BF16),
        pltpu.VMEM((K * SLICE, CH), F32),
        pltpu.VMEM((K, SLICE, HALF), F32),
        pltpu.VMEM((K, SLICE, HALF), F32),
        pltpu.VMEM((GROUPS,) + piece, BF16),
        pltpu.VMEM((3,) + piece, BF16),
        pltpu.VMEM((4,) + piece, BF16),
        pltpu.VMEM((3,) + piece, BF16),
        pltpu.VMEM((K, SLICE, HALF), BF16),
        pltpu.VMEM((16, K, SLICE, HALF), BF16),
        pltpu.VMEM((16, 3, SLICE, CELLS), BF16),
        pltpu.VMEM((CH, CH), BF16),
        dma((7,)), dma((8,)), dma((8,)), dma, dma, dma((2,)), dma((2,)), dma((6,)), dma((6,)), dma, dma,
        dma((4,)), dma((4,)), dma((2,)),
        dma((3,)), dma, dma, dma, dma, dma((3,)), dma((2,)), dma((2,)), dma((2,)), dma((2,)),
        dma((2,)), dma,
    ]
    out, ig, dw = pl.pallas_call(
        kernel,
        out_shape=(
            jax.ShapeDtypeStruct((ROWS, COLS, CH), BF16),
            jax.ShapeDtypeStruct((ROWS, COLS, CH), BF16),
            jax.ShapeDtypeStruct((K, CH, CH), BF16),
        ),
        in_specs=[hbm] * 7,
        out_specs=(vmem, vmem, vmem),
        scratch_shapes=scratch,
        compiler_params=pltpu.CompilerParams(collective_id=0, has_side_effects=True, vmem_limit_bytes=56 << 20),
    )(
        inputs, out_grad.reshape(CELLS, CH), weight, kernel_basis.transpose(1, 2, 0, 3),
        band_start, band_width, lon_reach,
    )
    return pl.pallas_call(
        finish,
        out_shape=(
            jax.ShapeDtypeStruct((ROWS, COLS, CH), BF16),
            jax.ShapeDtypeStruct((ROWS, COLS, CH), BF16),
            jax.ShapeDtypeStruct((K, CH, CH), F32),
        ),
        in_specs=[vmem] * 3,
        out_specs=(hbm, hbm, hbm),
        scratch_shapes=[pltpu.VMEM((K, CH, CH), F32), dma((2 + K,))],
        compiler_params=pltpu.CompilerParams(vmem_limit_bytes=56 << 20),
    )(out, ig, dw)


def solution(mesh):
    placed = (
        P("lat", "lon", None),
        P("lat", "lon", None),
        P(),
        P("lat", None, None, None),
        P("lat"),
        P("lat"),
        P("lat"),
    )
    return jax.shard_map(
        on_device,
        mesh=mesh,
        in_specs=placed,
        out_specs=(P("lat", "lon", None), P("lat", "lon", None), P()),
        check_vma=False,
    )
```

```python
import functools
import math

import jax
import jax.numpy as jnp
from jax import lax
from jax.experimental import pallas as pl
from jax.experimental.pallas import tpu as pltpu
from jax.sharding import PartitionSpec as P

MESH = pl.DeviceIdType.MESH
F32, BF16 = jnp.float32, jnp.bfloat16

ROWS, COLS, CH = 8, 16, 256
CELLS = ROWS * COLS
K, BAND, LONW = 9, 17, 33
EXT = 3 * ROWS
PITCH = 64
FLAT = EXT * PITCH
PAIRS = EXT // 2
HALF = 128
GROUPS = 3
KG = K // GROUPS
SLICE = 16


def whole_wait(buf, sem):
    pltpu.make_async_copy(buf, buf, sem).wait()


def kernel(
    x_ref, g_ref, w_ref, kb_ref, start_ref, width_ref, reach_ref,
    out_ref, ig_ref, dw_ref,
    start_v, width_v, reach_v, wv, kbv, mask, kbs, comb, op,
    xh, xtc, xc, em, xt, gown, gs, mt, mgt, mid, lat_out, lat_in, lon_out, lon_in, dwp,
    zs, zb, zg, zgd, fin, dwv, dwt, sg, eye, outv, igv,
    lsem, xsend, xrecv, xa_s, xa_r, seam_s, seam_r, fsend, frecv, g_s, g_r, igsend, igrecv,
    z_s, z_r, zg_s, zg_r, fin_s, fin_r, ag_s, ag_r, fw_s, fw_r, sg_s, sg_r, osem,
):
    lat, lon = lax.axis_index("lat"), lax.axis_index("lon")
    core = lax.rem(lat, 2)
    zlo = lat // 2
    zhi = lon // 16
    rank = lax.rem(lon, 16)
    cgroup, ohalf = rank // 2, lax.rem(rank, 2)
    slot = ohalf * 8 + cgroup
    z4 = lax.rem(zlo, 4)
    zgroup = zhi * 2 + zlo // 4
    up, down = lat - 1, lat + 1
    has_up, has_down = lat > 0, lat < 15
    east, west = lax.rem(lon + 1, 32), lax.rem(lon + 31, 32)
    partner = (lat + 1 - 2 * core, lon)
    not_first, not_last = rank > 0, rank < 15

    def plane_peer(d):
        return (lat, zhi * 16 + lax.rem(rank + d, 16))

    olon = (1 - zhi) * 16 + rank

    def z4_peer(t, h):
        return ((zlo - z4 + t) * 2 + h, lon)

    def zfar_peer(t):
        return (((t % 2) * 4 + z4) * 2 + core, (t // 2) * 16 + rank)

    def remote(src, dst, ssem, rsem, dev):
        return pltpu.make_async_remote_copy(
            src_ref=src, dst_ref=dst, send_sem=ssem, recv_sem=rsem, device_id=dev, device_id_type=MESH
        )

    mid_rows, top, bottom = pl.ds(ROWS, ROWS), pl.ds(0, ROWS), pl.ds(2 * ROWS, ROWS)
    mid_cols, wcols, ecols = pl.ds(COLS, COLS), pl.ds(0, COLS), pl.ds(2 * COLS, COLS)

    local = [
        pltpu.make_async_copy(kb_ref, kbv, lsem.at[0]),
        pltpu.make_async_copy(start_ref, start_v, lsem.at[1]),
        pltpu.make_async_copy(width_ref, width_v, lsem.at[2]),
        pltpu.make_async_copy(reach_ref, reach_v, lsem.at[3]),
        pltpu.make_async_copy(g_ref.at[:, pl.ds(0, HALF)], gown.at[0], lsem.at[4]),
        pltpu.make_async_copy(w_ref, wv, lsem.at[5]),
        pltpu.make_async_copy(x_ref, xh.at[mid_rows, mid_cols], lsem.at[6]),
        pltpu.make_async_copy(g_ref.at[:, pl.ds(HALF, HALF)], gown.at[1], lsem.at[7]),
    ]
    for c in (local[6],) + tuple(local[:6]) + (local[7],):
        c.start()

    @pl.when(jnp.logical_not(has_up))
    def _():
        xh[0:ROWS] = jnp.zeros((ROWS, PITCH, CH), BF16)
        xc[0] = jnp.zeros((18, 2, SLICE, CELLS), BF16)
        lat_in[0] = jnp.zeros((ROWS, 3 * COLS, CH), BF16)

    @pl.when(jnp.logical_not(has_down))
    def _():
        xh[2 * ROWS : EXT] = jnp.zeros((ROWS, PITCH, CH), BF16)
        xc[2] = jnp.zeros((18, 2, SLICE, CELLS), BF16)
        lat_in[1] = jnp.zeros((ROWS, 3 * COLS, CH), BF16)

    bar = pltpu.get_barrier_semaphore()

    def signal(dev):
        pl.semaphore_signal(bar, inc=1, device_id=dev, device_id_type=MESH)

    for d in range(1, 4):
        signal(zfar_peer(lax.rem(zgroup + d, 4)))
    for d in range(1, 16):
        signal(plane_peer(d))
    for d in range(1, 4):
        for h in range(2):
            signal(z4_peer(lax.rem(z4 + d, 4), h))

    @pl.when(has_up)
    def _():
        signal((up, olon))
        signal((up, lon))

    @pl.when(has_down)
    def _():
        signal((down, olon))
        signal((down, lon))

    local[6].wait()
    xtc[...] = xh[mid_rows, mid_cols, :].reshape(CELLS, CH).astype(F32).T.astype(BF16).reshape(2, HALF, CELLS)

    def channels(group):
        return pl.ds(pl.multiple_of(group * SLICE, SLICE), SLICE)

    xc[1, 1 + rank] = xtc[:, channels(cgroup), :]

    kbs[...] = jnp.zeros_like(kbs)
    xh[:, 3 * COLS : PITCH] = jnp.zeros((EXT, PITCH - 3 * COLS, CH), BF16)
    eye[...] = (
        lax.broadcasted_iota(jnp.int32, (CH, CH), 0) == lax.broadcasted_iota(jnp.int32, (CH, CH), 1)
    ).astype(F32).astype(BF16)
    cell = lax.broadcasted_iota(jnp.int32, (3 * CELLS, ROWS * PITCH), 0)
    place = (cell % CELLS) // COLS * PITCH + cell // CELLS * COLS + cell % COLS
    em[...] = (place == lax.broadcasted_iota(jnp.int32, (3 * CELLS, ROWS * PITCH), 1)).astype(F32).astype(BF16)

    for c in local[:4]:
        c.wait()
    row = lax.broadcasted_iota(jnp.int32, (BAND, ROWS, LONW), 1)
    band_pos = lax.broadcasted_iota(jnp.int32, (BAND, ROWS, LONW), 0)
    lon_off = jnp.abs(lax.broadcasted_iota(jnp.int32, (BAND, ROWS, LONW), 2) - (LONW - 1) // 2)
    inside = jnp.zeros((BAND, ROWS, LONW), jnp.bool_)
    for i in range(ROWS):
        first = start_v[i]
        keep = (band_pos >= first) & (band_pos < first + width_v[i]) & (lon_off <= reach_v[i])
        inside = inside | (keep & (row == i))
    mask[...] = inside.astype(F32)

    def op_step(k, carry):
        kbs[1 : 1 + BAND, :, 0:LONW] = jnp.where(mask[...] > 0.5, kbv[k].astype(F32), 0.0)
        for t in range(BAND + 1):
            comb[t] = kbs[t] + pltpu.roll(kbs[t + 1], PITCH, 1)
        for i in range(ROWS):
            for q in range(PAIRS):
                t = 2 * q - i + 1
                if 0 <= t <= BAND:
                    line = jnp.broadcast_to(comb[t, i : i + 1, :], (COLS, 128))
                    tile = pltpu.roll(line, 0, 1, stride=1, stride_axis=0)
                    op[k, i * COLS : (i + 1) * COLS, q * 128 : (q + 1) * 128] = tile.astype(BF16)
                else:
                    op[k, i * COLS : (i + 1) * COLS, q * 128 : (q + 1) * 128] = jnp.zeros((COLS, 128), BF16)
        return carry

    lax.fori_loop(0, K, op_step, 0)

    pl.semaphore_wait(bar, 24 + 2 * (has_up.astype(jnp.int32) + has_down.astype(jnp.int32)))

    which = jnp.where(rank == 0, 0, jnp.where(rank == 15, 1, 2))
    for d in range(1, 16):
        peer = lax.rem(rank + d, 16)
        remote(xtc.at[:, channels(peer // 2), :], xc.at[1, 1 + rank], xa_s, xa_r.at[which], plane_peer(d)).start()
    local[4].wait()
    local[7].wait()
    gs[rank] = gown[ohalf]
    for d in range(1, 16):
        peer = lax.rem(rank + d, 16)
        remote(gown.at[lax.rem(peer, 2)], gs.at[rank], g_s, g_r, plane_peer(d)).start()

    def start_vertical(pair):
        @pl.when(has_up)
        def _():
            pair[0].start()

        @pl.when(has_down)
        def _():
            pair[1].start()

    def wait_vertical(pair):
        @pl.when(has_down)
        def _():
            pair[0].wait_recv()

        @pl.when(has_up)
        def _():
            pair[1].wait_recv()

    def forward(slots, s):
        src = xc.at[1, slots]
        return (
            remote(src, xc.at[2, slots], fsend.at[s], frecv.at[s], (up, lon)),
            remote(src, xc.at[0, slots], fsend.at[s + 1], frecv.at[s + 1], (down, lon)),
        )

    def seam(src_slot, dst_slot, n):
        src = xc.at[1, src_slot]
        return (
            remote(src, xc.at[2, dst_slot], seam_s.at[n], seam_r.at[n], (up, olon)),
            remote(src, xc.at[0, dst_slot], seam_s.at[n + 1], seam_r.at[n + 1], (down, olon)),
            remote(src, xc.at[1, dst_slot], seam_s.at[n + 2], seam_r.at[n + 2], (lat, olon)),
        )

    seams = (seam(16, 0, 0), seam(1, 17, 3))
    forwards = (forward(pl.ds(1, 16), 0),)

    @pl.when(not_first)
    def _():
        whole_wait(xc.at[1, 1], xa_r.at[0])

    start_vertical(seams[1])
    seams[1][2].start()

    @pl.when(not_last)
    def _():
        whole_wait(xc.at[1, 16], xa_r.at[1])

    start_vertical(seams[0])
    seams[0][2].start()
    at_end = jnp.logical_or(rank == 0, rank == 15)

    @pl.when(at_end)
    def _():
        whole_wait(xc.at[1, pl.ds(1, 14)], xa_r.at[2])

    @pl.when(jnp.logical_not(at_end))
    def _():
        whole_wait(xc.at[1, pl.ds(1, 13)], xa_r.at[2])

    start_vertical(forwards[0])

    to_east = remote(x_ref, xh.at[mid_rows, wcols], xsend.at[0], xrecv.at[0], (lat, east))
    to_west = remote(x_ref, xh.at[mid_rows, ecols], xsend.at[1], xrecv.at[1], (lat, west))

    @pl.when(not_last)
    def _():
        to_east.start()

    @pl.when(not_first)
    def _():
        to_west.start()

    local[5].wait()
    g = jnp.concatenate([gown[0], gown[1]], axis=1)

    for k in range(K):
        part = jnp.dot(g, wv[k], preferred_element_type=F32).astype(BF16)
        part = lax.dot_general(eye[...], part, (((1,), (1,)), ((), ())), preferred_element_type=F32)
        mgt[:, k * CELLS : (k + 1) * CELLS] = part.astype(BF16)

    for n in range(FLAT // 256):
        part = jnp.dot(
            mgt[...], op[:, :, n * 256 : (n + 1) * 256].reshape(K * CELLS, 256), preferred_element_type=F32
        )
        part = part.T.reshape(4, PITCH, CH)[:, : 3 * COLS]
        r = n * 4
        if r < ROWS:
            lat_out[0, r : r + 4] = part.astype(BF16)
        elif r < 2 * ROWS:
            mid[r - ROWS : r - ROWS + 4] = part
        else:
            lat_out[1, r - 2 * ROWS : r - 2 * ROWS + 4] = part.astype(BF16)

    ig_up = remote(lat_out.at[0], lat_in.at[1], igsend.at[0], igrecv.at[0], (up, lon))
    ig_down = remote(lat_out.at[1], lat_in.at[0], igsend.at[1], igrecv.at[1], (down, lon))
    start_vertical((ig_up, ig_down))

    def up_down(cols, s):
        src = xh.at[mid_rows, cols]
        return (
            remote(src, xh.at[bottom, cols], xsend.at[s], xrecv.at[s], (up, lon)),
            remote(src, xh.at[top, cols], xsend.at[s + 1], xrecv.at[s + 1], (down, lon)),
        )

    verticals = (up_down(mid_cols, 2), up_down(wcols, 4), up_down(ecols, 6))
    start_vertical(verticals[0])

    def windows(slots):
        blocks = []
        for b in range(3):
            part = None
            for d in range(3):
                rows = [xc[b, a + d : a + d + n] for a, n in slots]
                rows = rows[0] if len(rows) == 1 else jnp.concatenate(rows, axis=0)
                term = jnp.dot(
                    rows.reshape(rows.shape[0] * 2 * SLICE, CELLS), em[d * CELLS : (d + 1) * CELLS],
                    preferred_element_type=F32,
                )
                part = term if part is None else part + term
            blocks.append(part.astype(BF16))
        return blocks

    def mixed(x, sectors):
        for s in range(GROUPS):
            part = lax.dot_general(
                x, op[s * KG : (s + 1) * KG].reshape(KG * CELLS, FLAT), (((1,), (1,)), ((), ())),
                preferred_element_type=F32,
            ).astype(BF16)
            for k in range(KG):
                for n, t in enumerate(sectors):
                    mt[s * KG + k, :, t * CELLS : (t + 1) * CELLS] = part[
                        n * 2 * SLICE : (n + 1) * 2 * SLICE, k * CELLS : (k + 1) * CELLS
                    ]

    def grad_term(a, n):
        return jnp.dot(
            mt[:, :, a * CELLS : (a + n) * CELLS].reshape(K * 2 * SLICE, n * CELLS),
            gs[a : a + n].reshape(n * CELLS, HALF),
            preferred_element_type=F32,
        )

    wait_vertical(forwards[0])
    for b, block in enumerate(windows(((1, 14),))):
        xt[:, b * ROWS * PITCH : (b + 1) * ROWS * PITCH] = block
    mixed(xt[...], range(1, 15))
    whole_wait(gs.at[pl.ds(0, 15)], g_r)
    dwp[...] = grad_term(1, 14)

    wait_vertical((ig_up, ig_down))
    total = mid[...] + lat_in[0].astype(F32) + lat_in[1].astype(F32)
    lon_out[0] = total[:, 0:COLS].astype(BF16)
    lon_out[1] = total[:, 2 * COLS : 3 * COLS].astype(BF16)
    mid[:, COLS : 2 * COLS] = total[:, COLS : 2 * COLS]
    ig_west = remote(lon_out.at[0], lon_in.at[1], igsend.at[2], igrecv.at[2], (lat, west))
    ig_east = remote(lon_out.at[1], lon_in.at[0], igsend.at[3], igrecv.at[3], (lat, east))
    for trio in seams:
        trio[2].wait_recv()
        wait_vertical(trio)
    for b, block in enumerate(windows(((0, 1), (15, 1)))):
        xt[0 : 4 * SLICE, b * ROWS * PITCH : (b + 1) * ROWS * PITCH] = block
    mixed(xt[0 : 4 * SLICE, :], (0, 15))
    scale = 1.0 / math.sqrt(CELLS * 512)
    term = (dwp[...] + grad_term(0, 1) + grad_term(15, 1)) * scale
    term = term.reshape(K, 2, SLICE, HALF)

    for s in range(GROUPS):
        for h in range(2):
            zs[s, h] = term[s * KG : (s + 1) * KG, h].astype(BF16)

            @pl.when(jnp.logical_or(z4 != s, core != h))
            def _():
                place = lax.rem(z4 - s + 4, 4) * 2 + lax.rem(core - h + 2, 2) - 1
                remote(zs.at[s, h], zb.at[place], z_s.at[2 * s + h], z_r, z4_peer(s, h)).start()

    ig_west.start()
    ig_east.start()

    to_first = remote(xc.at[:, 0, ohalf], sg.at[slot], sg_s.at[0], sg_r, (lat, zhi * 16))
    to_last = remote(xc.at[:, 17, ohalf], sg.at[slot], sg_s.at[1], sg_r, (lat, zhi * 16 + 15))

    @pl.when(not_first)
    def _():
        to_first.start()
        to_east.wait_recv()
        start_vertical(verticals[1])

    @pl.when(not_last)
    def _():
        to_last.start()
        to_west.wait_recv()
        start_vertical(verticals[2])

    @pl.when(z4 < GROUPS)
    def _():
        whole_wait(zb, z_r)
        part = zs[z4, core].astype(F32)
        for d in range(7):
            part += zb[d].astype(F32)
        zg[zgroup] = part.astype(BF16)
        for d in range(1, 4):
            remote(
                zg.at[zgroup], zg.at[zgroup], zg_s, zg_r, zfar_peer(lax.rem(zgroup + d, 4))
            ).start()

    @pl.when(z4 < GROUPS)
    def _():
        whole_wait(zgd, zg_r)
        part = zg[0].astype(F32)
        for d in range(1, 4):
            part += zg[d].astype(F32)
        mine = pl.ds(z4 * KG, KG)
        fin[mine] = part.astype(BF16)
        for d in range(1, 4):
            remote(fin.at[mine], fin.at[mine], fin_s, fin_r.at[z4], z4_peer(lax.rem(z4 + d, 4), core)).start()

    parts = (pl.ds(0, 2 * KG), pl.ds(2 * KG, KG))
    for s in range(GROUPS):
        @pl.when(z4 != s)
        def _():
            whole_wait(fin.at[pl.ds(s * KG, KG)], fin_r.at[s])

        if s == 0:
            continue
        ks = parts[s - 1]
        for d in range(1, 16):
            remote(fin.at[ks], dwv.at[slot, ks], ag_s.at[s - 1], ag_r.at[s - 1], plane_peer(d)).start()
        dwv[slot, ks] = fin[ks]

    wait_vertical(verticals[0])

    def from_sectors(sector, cols):
        whole_wait(sg.at[pl.ds(0, 15)], sg_r)
        sg[slot] = xc[:, sector, ohalf]
        for b in range(3):
            block = sg[:, b].reshape(CH, CELLS).astype(F32).T.astype(BF16)
            xh[b * ROWS : (b + 1) * ROWS, cols, :] = block.reshape(ROWS, COLS, CH)

    @pl.when(not_first)
    def _():
        wait_vertical(verticals[1])

    @pl.when(not_last)
    def _():
        wait_vertical(verticals[2])

    @pl.when(rank == 0)
    def _():
        from_sectors(0, wcols)

    @pl.when(rank == 15)
    def _():
        from_sectors(17, ecols)

    flat_x = xh[...].reshape(FLAT, CH)
    acc = jnp.zeros((CELLS, CH), F32)
    for s in range(GROUPS):
        m = jnp.dot(op[s * KG : (s + 1) * KG].reshape(KG * CELLS, FLAT), flat_x, preferred_element_type=F32)
        m = m.astype(BF16).reshape(KG, CELLS, CH)
        for k in range(KG):
            acc += lax.dot_general(m[k], wv[s * KG + k], (((1,), (1,)), ((), ())), preferred_element_type=F32)
    outv[...] = acc.astype(BF16).reshape(ROWS, COLS, CH)
    tails = [pltpu.make_async_copy(outv, out_ref, osem.at[0])]
    tails[0].start()

    ig_east.wait_recv()
    ig_west.wait_recv()
    total = mid[:, COLS : 2 * COLS] + lon_in[0].astype(F32) + lon_in[1].astype(F32)
    igv[...] = total.astype(BF16)
    tails.append(pltpu.make_async_copy(igv, ig_ref, osem.at[1]))
    tails[1].start()

    half = pl.ds(pl.multiple_of(core * HALF, HALF), HALF)
    small_eye = eye[0:HALF, 0:HALF]
    for s, ks in enumerate(parts):
        whole_wait(dwv.at[pl.ds(0, 15), ks], ag_r.at[s])
        for k in range(ks.start, ks.start + ks.size):
            for h in range(2):
                block = dwv[8 * h : 8 * h + 8, k].reshape(HALF, HALF)
                part = lax.dot_general(small_eye, block, (((1,), (1,)), ((), ())), preferred_element_type=F32)
                dwt[k, h * HALF : (h + 1) * HALF, :] = part.astype(BF16)
        tails.append(remote(dwt.at[ks], dw_ref.at[ks, :, half], fw_s.at[s], fw_r.at[s], partner))
        tails.append(pltpu.make_async_copy(dwt.at[ks], dw_ref.at[ks, :, half], osem.at[2 + s]))
        tails[-2].start()
        tails[-1].start()

    for s, ks in enumerate(parts):
        whole_wait(dwv.at[pl.ds(0, 15), ks], ag_s.at[s])

    for s in range(GROUPS):
        for h in range(2):
            @pl.when(jnp.logical_or(z4 != s, core != h))
            def _():
                whole_wait(zs.at[s, h], z_s.at[2 * s + h])

    @pl.when(z4 < GROUPS)
    def _():
        whole_wait(zgd, zg_s)
        whole_wait(zgd, fin_s)

    whole_wait(xc.at[1, pl.ds(1, 15)], xa_s)
    whole_wait(gs.at[pl.ds(0, 15)], g_s)
    ig_east.wait_send()
    ig_west.wait_send()

    for trio in seams:
        trio[2].wait_send()

    def sent_vertical(pairs):
        @pl.when(has_up)
        def _():
            for pair in pairs:
                pair[0].wait_send()

        @pl.when(has_down)
        def _():
            for pair in pairs:
                pair[1].wait_send()

    sent_vertical(forwards + seams + ((ig_up, ig_down), verticals[0]))

    @pl.when(not_first)
    def _():
        to_first.wait_send()
        to_west.wait_send()
        sent_vertical(verticals[1:2])

    @pl.when(not_last)
    def _():
        to_last.wait_send()
        to_east.wait_send()
        sent_vertical(verticals[2:3])

    for c in tails:
        c.wait()


def finish(out_ref, ig_ref, dw_ref, out_hbm, ig_hbm, dw_hbm, small, narrow, wide, sems):
    loads = [pltpu.make_async_copy(dw_ref.at[k], narrow.at[k], sems.at[k]) for k in range(K)]
    loads += [
        pltpu.make_async_copy(out_ref, small.at[0], sems.at[K]),
        pltpu.make_async_copy(ig_ref, small.at[1], sems.at[K + 1]),
    ]
    stores = [pltpu.make_async_copy(wide.at[k], dw_hbm.at[k], sems.at[K + 2 + k]) for k in range(K)]
    stores += [
        pltpu.make_async_copy(small.at[0], out_hbm, sems.at[2 * K + 2]),
        pltpu.make_async_copy(small.at[1], ig_hbm, sems.at[2 * K + 3]),
    ]
    for c in loads:
        c.start()
    for k in range(K + 2):
        loads[k].wait()
        if k < K:
            wide[k] = narrow[k].astype(F32)
        stores[k].start()
    for c in stores:
        c.wait()


def on_device(inputs, out_grad, weight, kernel_basis, band_start, band_width, lon_reach):
    hbm = pl.BlockSpec(memory_space=pltpu.HBM)
    dma = pltpu.SemaphoreType.DMA
    piece = (KG, SLICE, HALF)
    scratch = [
        pltpu.SMEM((ROWS,), jnp.int32),
        pltpu.SMEM((ROWS,), jnp.int32),
        pltpu.SMEM((ROWS,), jnp.int32),
        pltpu.VMEM((K, CH, CH), BF16),
        pltpu.VMEM((K, BAND, ROWS, LONW), BF16),
        pltpu.VMEM((BAND, ROWS, LONW), F32),
        pltpu.VMEM((BAND + 2, ROWS, 128), F32),
        pltpu.VMEM((BAND + 1, ROWS, 128), F32),
        pltpu.VMEM((K, CELLS, FLAT), BF16),
        pltpu.VMEM((EXT, PITCH, CH), BF16),
        pltpu.VMEM((2, HALF, CELLS), BF16),
        pltpu.VMEM((3, 18, 2, SLICE, CELLS), BF16),
        pltpu.VMEM((3 * CELLS, ROWS * PITCH), BF16),
        pltpu.VMEM((28 * SLICE, FLAT), BF16),
        pltpu.VMEM((2, CELLS, HALF), BF16),
        pltpu.VMEM((16, CELLS, HALF), BF16),
        pltpu.VMEM((K, 2 * SLICE, 16 * CELLS), BF16),
        pltpu.VMEM((CH, K * CELLS), BF16),
        pltpu.VMEM((ROWS, 3 * COLS, CH), F32),
        pltpu.VMEM((2, ROWS, 3 * COLS, CH), BF16),
        pltpu.VMEM((2, ROWS, 3 * COLS, CH), BF16),
        pltpu.VMEM((2, ROWS, COLS, CH), BF16),
        pltpu.VMEM((2, ROWS, COLS, CH), BF16),
        pltpu.VMEM((K * 2 * SLICE, HALF), F32),
        pltpu.VMEM((GROUPS, 2) + piece, BF16),
        pltpu.VMEM((7,) + piece, BF16),
        pltpu.VMEM((4,) + piece, BF16),
        pltpu.VMEM((3,) + piece, BF16),
        pltpu.VMEM((K, SLICE, HALF), BF16),
        pltpu.VMEM((16, K, SLICE, HALF), BF16),
        pltpu.VMEM((K, CH, HALF), BF16),
        pltpu.VMEM((16, 3, SLICE, CELLS), BF16),
        pltpu.VMEM((CH, CH), BF16),
        pltpu.VMEM((ROWS, COLS, CH), BF16),
        pltpu.VMEM((ROWS, COLS, CH), BF16),
        dma((8,)), dma((8,)), dma((8,)), dma, dma((3,)), dma((6,)), dma((6,)), dma((2,)), dma((2,)), dma, dma,
        dma((4,)), dma((4,)),
        dma((6,)), dma, dma, dma, dma, dma((3,)), dma((2,)), dma((2,)), dma((2,)), dma((2,)), dma((2,)), dma, dma((4,)),
    ]
    out, ig, dw = pl.pallas_call(
        kernel,
        out_shape=(
            jax.ShapeDtypeStruct((ROWS, COLS, CH), BF16),
            jax.ShapeDtypeStruct((ROWS, COLS, CH), BF16),
            jax.ShapeDtypeStruct((K, CH, CH), BF16),
        ),
        in_specs=[hbm] * 7,
        out_specs=(hbm, hbm, hbm),
        scratch_shapes=scratch,
        compiler_params=pltpu.CompilerParams(collective_id=0, has_side_effects=True, vmem_limit_bytes=56 << 20),
    )(
        inputs, out_grad.reshape(CELLS, CH), weight, kernel_basis.transpose(1, 2, 0, 3),
        band_start, band_width, lon_reach,
    )
    return pl.pallas_call(
        finish,
        out_shape=(
            jax.ShapeDtypeStruct((ROWS, COLS, CH), BF16),
            jax.ShapeDtypeStruct((ROWS, COLS, CH), BF16),
            jax.ShapeDtypeStruct((K, CH, CH), F32),
        ),
        in_specs=[hbm] * 3,
        out_specs=(hbm, hbm, hbm),
        scratch_shapes=[
            pltpu.VMEM((2, ROWS, COLS, CH), BF16),
            pltpu.VMEM((K, CH, CH), BF16),
            pltpu.VMEM((K, CH, CH), F32),
            dma((2 * K + 4,)),
        ],
        compiler_params=pltpu.CompilerParams(vmem_limit_bytes=56 << 20),
    )(out, ig, dw)


def solution(mesh):
    placed = (
        P("lat", "lon", None),
        P("lat", "lon", None),
        P(),
        P("lat", None, None, None),
        P("lat"),
        P("lat"),
        P("lat"),
    )
    return jax.shard_map(
        on_device,
        mesh=mesh,
        in_specs=placed,
        out_specs=(P("lat", "lon", None), P("lat", "lon", None), P()),
        check_vma=False,
    )
```

```python
import functools
import math

import jax
import jax.numpy as jnp
from jax import lax
from jax.experimental import pallas as pl
from jax.experimental.pallas import tpu as pltpu
from jax.sharding import PartitionSpec as P

MESH = pl.DeviceIdType.MESH
F32, BF16 = jnp.float32, jnp.bfloat16

ROWS, COLS, CH = 8, 16, 256
CELLS = ROWS * COLS
K, BAND, LONW = 9, 17, 33
EXT = 3 * ROWS
PITCH = 64
FLAT = EXT * PITCH
PAIRS = EXT // 2
HALF = 128
GROUPS = 3
OWNERS = 4
FINAL = ((0, 3), (3, 5), (5, 7), (7, 9))
REST = (((3, 7), (7, 9)), ((0, 3), (5, 9)), ((0, 5), (7, 9)), ((0, 4), (4, 7)))
KG = K // GROUPS
SLICE = 16


def whole_wait(buf, sem):
    pltpu.make_async_copy(buf, buf, sem).wait()


def kernel(
    x_ref, g_ref, w_ref, kb_ref, start_ref, width_ref, reach_ref,
    out_ref, ig_ref, dw_ref,
    start_v, width_v, reach_v, wv, kbv, mask, kbs, comb, op,
    xh, xtc, xc, em, xt, gown, gs, mt, mgt, mid, lat_out, lat_in, lon_out, lon_in, dwp,
    zs, zb, zg, zgd, finb, fin, dwv, sg, eye,
    lsem, xsend, xrecv, xa_s, xa_r, seam_s, seam_r, fsend, frecv, g_s, g_r, igsend, igrecv,
    z_s, z_r, zg_s, zg_r, fin_s, fin_r, ag_s, ag_r, fw_s, fw_r, sg_s, sg_r,
):
    lat, lon = lax.axis_index("lat"), lax.axis_index("lon")
    core = lax.rem(lat, 2)
    zlo = lat // 2
    zhi = lon // 16
    rank = lax.rem(lon, 16)
    cgroup, ohalf = rank // 2, lax.rem(rank, 2)
    slot = ohalf * 8 + cgroup
    z4 = lax.rem(zlo, 4)
    zgroup = zhi * 2 + zlo // 4
    up, down = lat - 1, lat + 1
    has_up, has_down = lat > 0, lat < 15
    east, west = lax.rem(lon + 1, 32), lax.rem(lon + 31, 32)
    partner = (lat + 1 - 2 * core, lon)
    not_first, not_last = rank > 0, rank < 15

    def plane_peer(d):
        return (lat, zhi * 16 + lax.rem(rank + d, 16))

    olon = (1 - zhi) * 16 + rank

    def z4_peer(t, h):
        return ((zlo - z4 + t) * 2 + h, lon)

    def zfar_peer(t):
        return (((t % 2) * 4 + z4) * 2 + core, (t // 2) * 16 + rank)

    def remote(src, dst, ssem, rsem, dev):
        return pltpu.make_async_remote_copy(
            src_ref=src, dst_ref=dst, send_sem=ssem, recv_sem=rsem, device_id=dev, device_id_type=MESH
        )

    mid_rows, top, bottom = pl.ds(ROWS, ROWS), pl.ds(0, ROWS), pl.ds(2 * ROWS, ROWS)
    mid_cols, wcols, ecols = pl.ds(COLS, COLS), pl.ds(0, COLS), pl.ds(2 * COLS, COLS)

    local = [
        pltpu.make_async_copy(kb_ref, kbv, lsem.at[0]),
        pltpu.make_async_copy(start_ref, start_v, lsem.at[1]),
        pltpu.make_async_copy(width_ref, width_v, lsem.at[2]),
        pltpu.make_async_copy(reach_ref, reach_v, lsem.at[3]),
        pltpu.make_async_copy(g_ref.at[:, pl.ds(0, HALF)], gown.at[0], lsem.at[4]),
        pltpu.make_async_copy(w_ref, wv, lsem.at[5]),
        pltpu.make_async_copy(x_ref, xh.at[mid_rows, mid_cols], lsem.at[6]),
        pltpu.make_async_copy(g_ref.at[:, pl.ds(HALF, HALF)], gown.at[1], lsem.at[7]),
    ]
    for c in (local[6],) + tuple(local[:6]) + (local[7],):
        c.start()

    @pl.when(jnp.logical_not(has_up))
    def _():
        xh[0:ROWS] = jnp.zeros((ROWS, PITCH, CH), BF16)
        xc[0] = jnp.zeros((18, 2, SLICE, CELLS), BF16)
        lat_in[0] = jnp.zeros((ROWS, 3 * COLS, CH), BF16)

    @pl.when(jnp.logical_not(has_down))
    def _():
        xh[2 * ROWS : EXT] = jnp.zeros((ROWS, PITCH, CH), BF16)
        xc[2] = jnp.zeros((18, 2, SLICE, CELLS), BF16)
        lat_in[1] = jnp.zeros((ROWS, 3 * COLS, CH), BF16)

    bar = pltpu.get_barrier_semaphore()

    def signal(dev):
        pl.semaphore_signal(bar, inc=1, device_id=dev, device_id_type=MESH)

    for d in range(1, 4):
        signal(zfar_peer(lax.rem(zgroup + d, 4)))
    for d in range(1, 16):
        signal(plane_peer(d))
    for d in range(1, 4):
        for h in range(2):
            signal(z4_peer(lax.rem(z4 + d, 4), h))

    @pl.when(has_up)
    def _():
        signal((up, olon))
        signal((up, lon))

    @pl.when(has_down)
    def _():
        signal((down, olon))
        signal((down, lon))

    local[6].wait()
    xtc[...] = xh[mid_rows, mid_cols, :].reshape(CELLS, CH).astype(F32).T.astype(BF16).reshape(2, HALF, CELLS)

    def channels(group):
        return pl.ds(pl.multiple_of(group * SLICE, SLICE), SLICE)

    xc[1, 1 + rank] = xtc[:, channels(cgroup), :]

    kbs[...] = jnp.zeros_like(kbs)
    xh[:, 3 * COLS : PITCH] = jnp.zeros((EXT, PITCH - 3 * COLS, CH), BF16)
    eye[...] = (
        lax.broadcasted_iota(jnp.int32, (CH, CH), 0) == lax.broadcasted_iota(jnp.int32, (CH, CH), 1)
    ).astype(F32).astype(BF16)
    cell = lax.broadcasted_iota(jnp.int32, (3 * CELLS, ROWS * PITCH), 0)
    place = (cell % CELLS) // COLS * PITCH + cell // CELLS * COLS + cell % COLS
    em[...] = (place == lax.broadcasted_iota(jnp.int32, (3 * CELLS, ROWS * PITCH), 1)).astype(F32).astype(BF16)

    for c in local[:4]:
        c.wait()
    row = lax.broadcasted_iota(jnp.int32, (BAND, ROWS, LONW), 1)
    band_pos = lax.broadcasted_iota(jnp.int32, (BAND, ROWS, LONW), 0)
    lon_off = jnp.abs(lax.broadcasted_iota(jnp.int32, (BAND, ROWS, LONW), 2) - (LONW - 1) // 2)
    inside = jnp.zeros((BAND, ROWS, LONW), jnp.bool_)
    for i in range(ROWS):
        first = start_v[i]
        keep = (band_pos >= first) & (band_pos < first + width_v[i]) & (lon_off <= reach_v[i])
        inside = inside | (keep & (row == i))
    mask[...] = inside.astype(F32)

    def op_step(k, carry):
        kbs[1 : 1 + BAND, :, 0:LONW] = jnp.where(mask[...] > 0.5, kbv[k].astype(F32), 0.0)
        for t in range(BAND + 1):
            comb[t] = kbs[t] + pltpu.roll(kbs[t + 1], PITCH, 1)
        for i in range(ROWS):
            for q in range(PAIRS):
                t = 2 * q - i + 1
                if 0 <= t <= BAND:
                    line = jnp.broadcast_to(comb[t, i : i + 1, :], (COLS, 128))
                    tile = pltpu.roll(line, 0, 1, stride=1, stride_axis=0)
                    op[k, i * COLS : (i + 1) * COLS, q * 128 : (q + 1) * 128] = tile.astype(BF16)
                else:
                    op[k, i * COLS : (i + 1) * COLS, q * 128 : (q + 1) * 128] = jnp.zeros((COLS, 128), BF16)
        return carry

    lax.fori_loop(0, K, op_step, 0)

    pl.semaphore_wait(bar, 24 + 2 * (has_up.astype(jnp.int32) + has_down.astype(jnp.int32)))

    which = jnp.where(rank == 0, 0, jnp.where(rank == 15, 1, 2))
    for d in range(1, 16):
        peer = lax.rem(rank + d, 16)
        remote(xtc.at[:, channels(peer // 2), :], xc.at[1, 1 + rank], xa_s, xa_r.at[which], plane_peer(d)).start()
    local[4].wait()
    local[7].wait()
    gs[rank] = gown[ohalf]
    for d in range(1, 16):
        peer = lax.rem(rank + d, 16)
        remote(gown.at[lax.rem(peer, 2)], gs.at[rank], g_s, g_r, plane_peer(d)).start()

    def start_vertical(pair):
        @pl.when(has_up)
        def _():
            pair[0].start()

        @pl.when(has_down)
        def _():
            pair[1].start()

    def wait_vertical(pair):
        @pl.when(has_down)
        def _():
            pair[0].wait_recv()

        @pl.when(has_up)
        def _():
            pair[1].wait_recv()

    def forward(slots, s):
        src = xc.at[1, slots]
        return (
            remote(src, xc.at[2, slots], fsend.at[s], frecv.at[s], (up, lon)),
            remote(src, xc.at[0, slots], fsend.at[s + 1], frecv.at[s + 1], (down, lon)),
        )

    def seam(src_slot, dst_slot, n):
        src = xc.at[1, src_slot]
        return (
            remote(src, xc.at[2, dst_slot], seam_s.at[n], seam_r.at[n], (up, olon)),
            remote(src, xc.at[0, dst_slot], seam_s.at[n + 1], seam_r.at[n + 1], (down, olon)),
            remote(src, xc.at[1, dst_slot], seam_s.at[n + 2], seam_r.at[n + 2], (lat, olon)),
        )

    seams = (seam(16, 0, 0), seam(1, 17, 3))
    forwards = (forward(pl.ds(1, 16), 0),)

    @pl.when(not_first)
    def _():
        whole_wait(xc.at[1, 1], xa_r.at[0])

    start_vertical(seams[1])
    seams[1][2].start()

    @pl.when(not_last)
    def _():
        whole_wait(xc.at[1, 16], xa_r.at[1])

    start_vertical(seams[0])
    seams[0][2].start()
    at_end = jnp.logical_or(rank == 0, rank == 15)

    @pl.when(at_end)
    def _():
        whole_wait(xc.at[1, pl.ds(1, 14)], xa_r.at[2])

    @pl.when(jnp.logical_not(at_end))
    def _():
        whole_wait(xc.at[1, pl.ds(1, 13)], xa_r.at[2])

    start_vertical(forwards[0])

    to_east = remote(x_ref, xh.at[mid_rows, wcols], xsend.at[0], xrecv.at[0], (lat, east))
    to_west = remote(x_ref, xh.at[mid_rows, ecols], xsend.at[1], xrecv.at[1], (lat, west))

    @pl.when(not_last)
    def _():
        to_east.start()

    @pl.when(not_first)
    def _():
        to_west.start()

    local[5].wait()
    g = jnp.concatenate([gown[0], gown[1]], axis=1)

    for k in range(K):
        part = jnp.dot(g, wv[k], preferred_element_type=F32).astype(BF16)
        part = lax.dot_general(eye[...], part, (((1,), (1,)), ((), ())), preferred_element_type=F32)
        mgt[:, k * CELLS : (k + 1) * CELLS] = part.astype(BF16)

    for n in range(FLAT // 256):
        part = jnp.dot(
            mgt[...], op[:, :, n * 256 : (n + 1) * 256].reshape(K * CELLS, 256), preferred_element_type=F32
        )
        part = part.T.reshape(4, PITCH, CH)[:, : 3 * COLS]
        r = n * 4
        if r < ROWS:
            lat_out[0, r : r + 4] = part.astype(BF16)
        elif r < 2 * ROWS:
            mid[r - ROWS : r - ROWS + 4] = part
        else:
            lat_out[1, r - 2 * ROWS : r - 2 * ROWS + 4] = part.astype(BF16)

    ig_up = remote(lat_out.at[0], lat_in.at[1], igsend.at[0], igrecv.at[0], (up, lon))
    ig_down = remote(lat_out.at[1], lat_in.at[0], igsend.at[1], igrecv.at[1], (down, lon))
    start_vertical((ig_up, ig_down))

    def up_down(cols, s):
        src = xh.at[mid_rows, cols]
        return (
            remote(src, xh.at[bottom, cols], xsend.at[s], xrecv.at[s], (up, lon)),
            remote(src, xh.at[top, cols], xsend.at[s + 1], xrecv.at[s + 1], (down, lon)),
        )

    verticals = (up_down(mid_cols, 2), up_down(wcols, 4), up_down(ecols, 6))
    start_vertical(verticals[0])

    def windows(slots):
        blocks = []
        for b in range(3):
            part = None
            for d in range(3):
                rows = [xc[b, a + d : a + d + n] for a, n in slots]
                rows = rows[0] if len(rows) == 1 else jnp.concatenate(rows, axis=0)
                term = jnp.dot(
                    rows.reshape(rows.shape[0] * 2 * SLICE, CELLS), em[d * CELLS : (d + 1) * CELLS],
                    preferred_element_type=F32,
                )
                part = term if part is None else part + term
            blocks.append(part.astype(BF16))
        return blocks

    def mixed(x, sectors):
        for s in range(GROUPS):
            part = lax.dot_general(
                x, op[s * KG : (s + 1) * KG].reshape(KG * CELLS, FLAT), (((1,), (1,)), ((), ())),
                preferred_element_type=F32,
            ).astype(BF16)
            for k in range(KG):
                for n, t in enumerate(sectors):
                    mt[s * KG + k, :, t * CELLS : (t + 1) * CELLS] = part[
                        n * 2 * SLICE : (n + 1) * 2 * SLICE, k * CELLS : (k + 1) * CELLS
                    ]

    def grad_term(a, n):
        return jnp.dot(
            mt[:, :, a * CELLS : (a + n) * CELLS].reshape(K * 2 * SLICE, n * CELLS),
            gs[a : a + n].reshape(n * CELLS, HALF),
            preferred_element_type=F32,
        )

    wait_vertical(forwards[0])
    for b, block in enumerate(windows(((1, 14),))):
        xt[:, b * ROWS * PITCH : (b + 1) * ROWS * PITCH] = block
    mixed(xt[...], range(1, 15))
    whole_wait(gs.at[pl.ds(0, 15)], g_r)
    dwp[...] = grad_term(1, 14)

    wait_vertical((ig_up, ig_down))
    total = mid[...] + lat_in[0].astype(F32) + lat_in[1].astype(F32)
    lon_out[0] = total[:, 0:COLS].astype(BF16)
    lon_out[1] = total[:, 2 * COLS : 3 * COLS].astype(BF16)
    mid[:, COLS : 2 * COLS] = total[:, COLS : 2 * COLS]
    ig_west = remote(lon_out.at[0], lon_in.at[1], igsend.at[2], igrecv.at[2], (lat, west))
    ig_east = remote(lon_out.at[1], lon_in.at[0], igsend.at[3], igrecv.at[3], (lat, east))
    for trio in seams:
        trio[2].wait_recv()
        wait_vertical(trio)
    for b, block in enumerate(windows(((0, 1), (15, 1)))):
        xt[0 : 4 * SLICE, b * ROWS * PITCH : (b + 1) * ROWS * PITCH] = block
    mixed(xt[0 : 4 * SLICE, :], (0, 15))
    scale = 1.0 / math.sqrt(CELLS * 512)
    term = (dwp[...] + grad_term(0, 1) + grad_term(15, 1)) * scale
    term = term.reshape(K, 2, SLICE, HALF)

    for s in range(OWNERS):
        for h in range(2):
            zs[s, h] = term[2 * s : 2 * s + KG, h].astype(BF16)

            @pl.when(jnp.logical_or(z4 != s, core != h))
            def _():
                place = lax.rem(z4 - s + 4, 4) * 2 + lax.rem(core - h + 2, 2) - 1
                remote(zs.at[s, h], zb.at[place], z_s.at[2 * s + h], z_r, z4_peer(s, h)).start()

    ig_west.start()
    ig_east.start()

    to_first = remote(xc.at[:, 0, ohalf], sg.at[slot], sg_s.at[0], sg_r, (lat, zhi * 16))
    to_last = remote(xc.at[:, 17, ohalf], sg.at[slot], sg_s.at[1], sg_r, (lat, zhi * 16 + 15))

    @pl.when(not_first)
    def _():
        to_first.start()
        to_east.wait_recv()
        start_vertical(verticals[1])

    @pl.when(not_last)
    def _():
        to_last.start()
        to_west.wait_recv()
        start_vertical(verticals[2])

    whole_wait(zb, z_r)
    part = zs[z4, core].astype(F32)
    for d in range(7):
        part += zb[d].astype(F32)
    zg[zgroup] = part.astype(BF16)
    for d in range(1, 4):
        remote(zg.at[zgroup], zg.at[zgroup], zg_s, zg_r, zfar_peer(lax.rem(zgroup + d, 4))).start()

    whole_wait(zgd, zg_r)
    part = zg[0].astype(F32)
    for d in range(1, 4):
        part += zg[d].astype(F32)
    finb[z4] = part.astype(BF16)

    def gather(lo, hi, n):
        ks = pl.ds(lo, hi - lo)
        for d in range(1, 16):
            remote(fin.at[ks], dwv.at[slot, ks], ag_s.at[n], ag_r.at[n], plane_peer(d)).start()
        dwv[slot, ks] = fin[ks]

    for d in range(1, 4):
        remote(finb.at[z4], finb.at[z4], fin_s, fin_r.at[z4], z4_peer(lax.rem(z4 + d, 4), core)).start()
    for s, (lo, hi) in enumerate(FINAL):
        @pl.when(z4 == s)
        def _():
            fin[lo:hi] = finb[s, lo - 2 * s : hi - 2 * s]
            gather(lo, hi, 0)

    for s, (lo, hi) in enumerate(FINAL):
        @pl.when(z4 != s)
        def _():
            whole_wait(finb.at[s], fin_r.at[s])
            fin[lo:hi] = finb[s, lo - 2 * s : hi - 2 * s]

    for s in range(OWNERS):
        @pl.when(z4 == s)
        def _():
            for n, (lo, hi) in enumerate(REST[s]):
                gather(lo, hi, 1 + n)

    wait_vertical(verticals[0])

    def from_sectors(sector, cols):
        whole_wait(sg.at[pl.ds(0, 15)], sg_r)
        sg[slot] = xc[:, sector, ohalf]
        for b in range(3):
            block = sg[:, b].reshape(CH, CELLS).astype(F32).T.astype(BF16)
            xh[b * ROWS : (b + 1) * ROWS, cols, :] = block.reshape(ROWS, COLS, CH)

    @pl.when(not_first)
    def _():
        wait_vertical(verticals[1])

    @pl.when(not_last)
    def _():
        wait_vertical(verticals[2])

    @pl.when(rank == 0)
    def _():
        from_sectors(0, wcols)

    @pl.when(rank == 15)
    def _():
        from_sectors(17, ecols)

    flat_x = xh[...].reshape(FLAT, CH)
    acc = jnp.zeros((CELLS, CH), F32)
    for s in range(GROUPS):
        m = jnp.dot(op[s * KG : (s + 1) * KG].reshape(KG * CELLS, FLAT), flat_x, preferred_element_type=F32)
        m = m.astype(BF16).reshape(KG, CELLS, CH)
        for k in range(KG):
            acc += lax.dot_general(m[k], wv[s * KG + k], (((1,), (1,)), ((), ())), preferred_element_type=F32)
    out_ref[...] = acc.astype(BF16).reshape(ROWS, COLS, CH)

    ig_east.wait_recv()
    ig_west.wait_recv()
    total = mid[:, COLS : 2 * COLS] + lon_in[0].astype(F32) + lon_in[1].astype(F32)
    ig_ref[...] = total.astype(BF16)

    small_eye = eye[0:HALF, 0:HALF]

    def hand_over(lo, hi, n):
        ks = pl.ds(lo, hi - lo)
        return remote(dw_ref.at[core, ks], dw_ref.at[core, ks], fw_s.at[n], fw_r.at[n], partner)

    for s in range(OWNERS):
        @pl.when(z4 == s)
        def _():
            for n, (lo, hi) in enumerate((FINAL[s],) + REST[s]):
                whole_wait(dwv.at[pl.ds(0, 15), pl.ds(lo, hi - lo)], ag_r.at[n])
                for k in range(lo, hi):
                    for h in range(2):
                        block = dwv[8 * h : 8 * h + 8, k].reshape(HALF, HALF)
                        part = lax.dot_general(small_eye, block, (((1,), (1,)), ((), ())), preferred_element_type=F32)
                        dw_ref[core, k, h * HALF : (h + 1) * HALF, :] = part.astype(BF16)
                hand_over(lo, hi, n).start()

    for s in range(OWNERS):
        for h in range(2):
            @pl.when(jnp.logical_or(z4 != s, core != h))
            def _():
                whole_wait(zs.at[s, h], z_s.at[2 * s + h])

    whole_wait(zgd, zg_s)
    whole_wait(zgd, fin_s)

    whole_wait(xc.at[1, pl.ds(1, 15)], xa_s)
    whole_wait(gs.at[pl.ds(0, 15)], g_s)
    ig_east.wait_send()
    ig_west.wait_send()

    for trio in seams:
        trio[2].wait_send()

    def sent_vertical(pairs):
        @pl.when(has_up)
        def _():
            for pair in pairs:
                pair[0].wait_send()

        @pl.when(has_down)
        def _():
            for pair in pairs:
                pair[1].wait_send()

    sent_vertical(forwards + seams + ((ig_up, ig_down), verticals[0]))

    @pl.when(not_first)
    def _():
        to_first.wait_send()
        to_west.wait_send()
        sent_vertical(verticals[1:2])

    @pl.when(not_last)
    def _():
        to_last.wait_send()
        to_east.wait_send()
        sent_vertical(verticals[2:3])

    for s in range(OWNERS):
        @pl.when(z4 == s)
        def _():
            for n, (lo, hi) in enumerate((FINAL[s],) + REST[s]):
                whole_wait(dwv.at[pl.ds(0, 15), pl.ds(lo, hi - lo)], ag_s.at[n])
                hand_over(lo, hi, n).wait()


def finish(out_ref, ig_ref, dw_ref, out_hbm, ig_hbm, dw_hbm, wide, sems):
    copies = [
        pltpu.make_async_copy(out_ref, out_hbm, sems.at[K]),
        pltpu.make_async_copy(ig_ref, ig_hbm, sems.at[K + 1]),
    ]
    for c in copies:
        c.start()
    for k in range(K):
        for h in range(2):
            wide[k, :, h * HALF : (h + 1) * HALF] = dw_ref[h, k].astype(F32)
        copies.append(pltpu.make_async_copy(wide.at[k], dw_hbm.at[k], sems.at[k]))
        copies[-1].start()
    for c in copies:
        c.wait()


def on_device(inputs, out_grad, weight, kernel_basis, band_start, band_width, lon_reach):
    vmem = pl.BlockSpec(memory_space=pltpu.VMEM)
    hbm = pl.BlockSpec(memory_space=pltpu.HBM)
    dma = pltpu.SemaphoreType.DMA
    piece = (KG, SLICE, HALF)
    scratch = [
        pltpu.SMEM((ROWS,), jnp.int32),
        pltpu.SMEM((ROWS,), jnp.int32),
        pltpu.SMEM((ROWS,), jnp.int32),
        pltpu.VMEM((K, CH, CH), BF16),
        pltpu.VMEM((K, BAND, ROWS, LONW), BF16),
        pltpu.VMEM((BAND, ROWS, LONW), F32),
        pltpu.VMEM((BAND + 2, ROWS, 128), F32),
        pltpu.VMEM((BAND + 1, ROWS, 128), F32),
        pltpu.VMEM((K, CELLS, FLAT), BF16),
        pltpu.VMEM((EXT, PITCH, CH), BF16),
        pltpu.VMEM((2, HALF, CELLS), BF16),
        pltpu.VMEM((3, 18, 2, SLICE, CELLS), BF16),
        pltpu.VMEM((3 * CELLS, ROWS * PITCH), BF16),
        pltpu.VMEM((28 * SLICE, FLAT), BF16),
        pltpu.VMEM((2, CELLS, HALF), BF16),
        pltpu.VMEM((16, CELLS, HALF), BF16),
        pltpu.VMEM((K, 2 * SLICE, 16 * CELLS), BF16),
        pltpu.VMEM((CH, K * CELLS), BF16),
        pltpu.VMEM((ROWS, 3 * COLS, CH), F32),
        pltpu.VMEM((2, ROWS, 3 * COLS, CH), BF16),
        pltpu.VMEM((2, ROWS, 3 * COLS, CH), BF16),
        pltpu.VMEM((2, ROWS, COLS, CH), BF16),
        pltpu.VMEM((2, ROWS, COLS, CH), BF16),
        pltpu.VMEM((K * 2 * SLICE, HALF), F32),
        pltpu.VMEM((OWNERS, 2) + piece, BF16),
        pltpu.VMEM((7,) + piece, BF16),
        pltpu.VMEM((4,) + piece, BF16),
        pltpu.VMEM((3,) + piece, BF16),
        pltpu.VMEM((OWNERS,) + piece, BF16),
        pltpu.VMEM((K, SLICE, HALF), BF16),
        pltpu.VMEM((16, K, SLICE, HALF), BF16),
        pltpu.VMEM((16, 3, SLICE, CELLS), BF16),
        pltpu.VMEM((CH, CH), BF16),
        dma((8,)), dma((8,)), dma((8,)), dma, dma((3,)), dma((6,)), dma((6,)), dma((2,)), dma((2,)), dma, dma,
        dma((4,)), dma((4,)),
        dma((8,)), dma, dma, dma, dma, dma((4,)), dma((3,)), dma((3,)), dma((3,)), dma((3,)), dma((2,)), dma,
    ]
    out, ig, dw = pl.pallas_call(
        kernel,
        out_shape=(
            pltpu.VMEM((ROWS, COLS, CH), BF16),
            pltpu.VMEM((ROWS, COLS, CH), BF16),
            pltpu.VMEM((2, K, CH, HALF), BF16),
        ),
        in_specs=[hbm] * 7,
        out_specs=(vmem, vmem, vmem),
        scratch_shapes=scratch,
        compiler_params=pltpu.CompilerParams(collective_id=0, has_side_effects=True, vmem_limit_bytes=56 << 20),
    )(
        inputs, out_grad.reshape(CELLS, CH), weight, kernel_basis.transpose(1, 2, 0, 3),
        band_start, band_width, lon_reach,
    )
    return pl.pallas_call(
        finish,
        out_shape=(
            jax.ShapeDtypeStruct((ROWS, COLS, CH), BF16),
            jax.ShapeDtypeStruct((ROWS, COLS, CH), BF16),
            jax.ShapeDtypeStruct((K, CH, CH), F32),
        ),
        in_specs=[vmem] * 3,
        out_specs=(hbm, hbm, hbm),
        scratch_shapes=[pltpu.VMEM((K, CH, CH), F32), dma((K + 2,))],
        compiler_params=pltpu.CompilerParams(vmem_limit_bytes=8 << 20),
    )(out, ig, dw)


def solution(mesh):
    placed = (
        P("lat", "lon", None),
        P("lat", "lon", None),
        P(),
        P("lat", None, None, None),
        P("lat"),
        P("lat"),
        P("lat"),
    )
    return jax.shard_map(
        on_device,
        mesh=mesh,
        in_specs=placed,
        out_specs=(P("lat", "lon", None), P("lat", "lon", None), P()),
        check_vma=False,
    )
```
